256 devices in a mesh: seq: 32 (over x, y, core), exp: 8 (over z).
Axes of the slice: x: 4, y: 4, z: 8, core: 2. Of those that a mesh axis runs over, the one named last changes fastest.
Arguments:
- tokens: bfloat16 [4096, 5120], P('seq', 'exp'), may hold values from -6 to 6
- out_grad: bfloat16 [4096, 5120], P('seq', 'exp'), may hold values from -0.59765625 to 0.59765625
- expert_ids: int32 [4096, 6], P('seq'), may hold values from 0 to 159, all different within a row; in each aligned block of 128 rows (0 to 127, 128 to 255, ...) at most 12 rows name the same one
- gates: bfloat16 [4096, 6], P('seq'), may hold values from 0.099609375 to 1
- w_gate: bfloat16 [32, 1536, 5120], P('seq', 'exp'), may hold values from -0.078125 to 0.078125
- w_up: bfloat16 [32, 1536, 5120], P('seq', 'exp'), may hold values from -0.078125 to 0.078125
- w_down: bfloat16 [32, 1536, 5120], P('seq', 'exp'), may hold values from -0.15625 to 0.15625
- shared_gate: bfloat16 [5120, 1536], P('seq', 'exp'), may hold values from -0.078125 to 0.078125
- shared_up: bfloat16 [5120, 1536], P('seq', 'exp'), may hold values from -0.078125 to 0.078125
- shared_down: bfloat16 [1536, 5120], P('exp', 'seq'), may hold values from -0.15625 to 0.15625
Outputs:
- token_grad: bfloat16 [4096, 5120], P('seq', 'exp')
- gate_grad: float32 [4096, 6], P('seq')
- grad_gate: bfloat16 [32, 1536, 5120], P('seq', 'exp')
- grad_up: bfloat16 [32, 1536, 5120], P('seq', 'exp')
- grad_down: bfloat16 [32, 1536, 5120], P('seq', 'exp')
- shared_grad_gate: bfloat16 [5120, 1536], P('seq', 'exp')
- shared_grad_up: bfloat16 [5120, 1536], P('seq', 'exp')
- shared_grad_down: bfloat16 [1536, 5120], P('exp', 'seq')
The draws below stay inside these ranges and needn't reach their ends.
Inputs may be any that keep to these rules, and one draw needn't show every extreme that they name: `expert_ids`: in each aligned block of 128 rows (the tokens of one index of seq) no id is named by more than 12 rows. Ids of 32 or more name experts outside the window and take no part.
All inputs are finite; a program needn't handle non-finite values.
Results may differ from the reference program's by a relative error of at most 0.02.
Values may be sent and summed in bfloat16 or wider, within the bound.
A program may use at most 128 MiB of HBM per device.

```python
import math
import jax
import jax.numpy as jnp
import numpy as np
from jax import lax

D = 5120
FF = 1536
FS = 1536
ALL_EXPERTS = 160
TOPK = 6
TOK = 128
MOST = 12
TOKENS = 4096
EXPERTS_WIN = 32
N_SEQ = 32
N_EXP = 8


def block_scale(own_key, extent, split, least, high):
    gain, own = 1.0, jax.random.fold_in(own_key, 6)
    for axis_at, blocks in split:
        heights = jnp.exp(jax.random.uniform(jax.random.fold_in(own, axis_at), (blocks,), jnp.float32, least / len(split), high / len(split)))
        gain = gain * jnp.repeat(heights, extent[axis_at] // blocks).reshape([-1 if axis == axis_at else 1 for axis in range(len(extent))])
    return gain


def routed_block(key, own, number, rows, count, top, most, skew):
    sequence = jax.random.permutation(key, count)
    crowded, common = load_shares(count, rows * top, most, skew, True), load_shares(count, rows * top, most, skew, False)
    places = jnp.arange(count)

    def named(lengths, offset_by):
        used = int((lengths > 0).sum())
        fixed = max(1, used // 4)
        passed = fixed + (places - fixed + offset_by * (used - fixed)) % max(1, count - fixed)
        return jnp.zeros((count,), jnp.int32).at[sequence[jnp.where(places < fixed, places, passed)]].set(jnp.asarray(lengths, jnp.int32))

    lengths = jnp.where(number % 4 == 0, named(crowded, number // 4), named(common, number - number // 4 - 1))
    mixed = jax.random.permutation(jax.random.fold_in(own, 3), count)
    donor, sink = mixed[0:count // 2 * 2:2], mixed[1:count // 2 * 2:2]
    margin = jnp.minimum(lengths[donor] - 1, most - lengths[sink]) // 2
    margin = jnp.where((donor == sequence[0]) | (sink == sequence[0]) | (lengths[sink] == 0), 0, jnp.maximum(margin, 0))
    passed = jax.random.randint(jax.random.fold_in(own, 4), (count // 2,), 0, 1 << 20) % (margin + 1)
    lengths = lengths.at[donor].add(-passed).at[sink].add(passed)
    items = jnp.searchsorted(jnp.cumsum(lengths), jnp.arange(rows * top), side="right").astype(jnp.int32)
    listing = items.reshape(top, rows).T
    listing = listing[jax.random.permutation(jax.random.fold_in(own, 1), rows)]
    offset_by = jax.random.randint(jax.random.fold_in(own, 2), (rows, 1), 0, top)
    return jnp.take_along_axis(listing, (jnp.arange(top)[None, :] + offset_by) % top, axis=1)


def load_shares(number_of, total, bound, skew, full):
    portions = [(1 << 20) // math.isqrt(grade ** skew) + 1 for grade in range(1, number_of + 1)]
    largest = bound if full else min(bound, max(-(-total // number_of), total * portions[0] // sum(portions)))
    least = 1 if total - largest >= number_of - 1 else 0
    given, surplus = [largest] + [least] * (number_of - 1), total - largest - least * (number_of - 1)
    while surplus > 0:
        movable = [i for i in range(1, number_of) if given[i] < largest] or [i for i in range(1, number_of) if given[i] < bound]
        whole, budget = sum([portions[i] for i in movable]), surplus
        for i in movable:
            more = min(bound - given[i], max(1, budget * portions[i] // whole), surplus)
            given[i] = given[i] + more
            surplus = surplus - more
    return np.array(given)


def bell_draw(key, extent, scale, reach, shards=(), kind=jnp.bfloat16):
    level = block_scale(key, extent, shards, -0.22, 0.18) if shards else 1.0
    entries = jax.random.normal(key, extent, jnp.float32) * scale * level
    return jnp.minimum(jnp.maximum(entries, -reach), reach).astype(kind)


def setup_inputs(seed: int = 0) -> dict:
    splits = jax.random.split(jax.random.key(seed), 11)
    tokens = bell_draw(splits[0], (TOKENS, D), 1.0, 6.0, ((0, 32), (1, 8)))
    out_grad = bell_draw(splits[1], (TOKENS, D), 0.1, 0.59765625, ((0, 32), (1, 8)))
    expert_ids_keys = jax.random.split(jax.random.fold_in(splits[2], 1), TOKENS // TOK)
    expert_ids_turns = jax.random.permutation(jax.random.fold_in(splits[2], 3), TOKENS // TOK)
    expert_ids = jax.vmap(lambda own, number: routed_block(jax.random.fold_in(splits[2], 2), own, number, TOK, ALL_EXPERTS, TOPK, MOST, 1))(expert_ids_keys, expert_ids_turns).reshape((TOKENS, TOPK))
    gates = jnp.clip(jnp.exp(math.log(1.0) - 2.306499 * jax.random.uniform(splits[3], (TOKENS, TOPK), jnp.float32) ** block_scale(splits[3], (TOKENS, TOPK), ((0, 32),), -0.2, 0.2)), 0.099609375, 1.0).astype(jnp.bfloat16)
    w_gate = bell_draw(splits[4], (EXPERTS_WIN, FF, D), D ** -0.5, 0.078125, ((0, 32), (1, 8)))
    w_up = bell_draw(splits[5], (EXPERTS_WIN, FF, D), D ** -0.5, 0.078125, ((0, 32), (1, 8)))
    w_down = bell_draw(splits[6], (EXPERTS_WIN, FF, D), FF ** -0.5, 0.15625, ((0, 32), (1, 8)))
    shared_gate = bell_draw(splits[7], (D, FS), D ** -0.5, 0.078125, ((0, 32), (1, 8)))
    shared_up = bell_draw(splits[8], (D, FS), D ** -0.5, 0.078125, ((0, 32), (1, 8)))
    shared_down = bell_draw(splits[9], (FS, D), FS ** -0.5, 0.15625, ((0, 8), (1, 32)))
    return dict(tokens=tokens, out_grad=out_grad, expert_ids=expert_ids, gates=gates, w_gate=w_gate, w_up=w_up, w_down=w_down, shared_gate=shared_gate, shared_up=shared_up, shared_down=shared_down)


def dot_rows(left, right):
    return lax.dot_general(left, right, (((0,), (0,)), ((), ())), preferred_element_type=jnp.float32)


def dot_last(left, right):
    return lax.dot_general(left, right, (((1,), (1,)), ((), ())), preferred_element_type=jnp.float32)


def silu_parts(value):
    sig = jax.nn.sigmoid(value)
    return value * sig, sig * (1.0 + value * (1.0 - sig))


def group_sum(grad_a, grad_b, weight_a, weight_b):
    count = grad_a.shape[0]
    width = grad_a.shape[1] // N_EXP
    left_a = grad_a.reshape(count, N_EXP, width).astype(jnp.float32)
    left_b = grad_b.reshape(count, N_EXP, width).astype(jnp.float32)
    right_a = weight_a.reshape(N_EXP, width, D).astype(jnp.float32)
    right_b = weight_b.reshape(N_EXP, width, D).astype(jnp.float32)
    parts = jnp.einsum("rsf,sfd->srd", left_a, right_a) + jnp.einsum("rsf,sfd->srd", left_b, right_b)
    return jnp.sum(parts.astype(jnp.bfloat16).astype(jnp.float32), axis=0)


def route_table(expert_ids):
    ids = expert_ids.reshape(N_SEQ, TOK * TOPK)
    window = jnp.arange(EXPERTS_WIN, dtype=jnp.int32)
    onehot = (ids[:, :, None] == window[None, None, :]).astype(jnp.int32)
    rank = jnp.sum((jnp.cumsum(onehot, axis=1) - onehot) * onehot, axis=2)
    block = jnp.arange(N_SEQ, dtype=jnp.int32)[:, None]
    dead = EXPERTS_WIN * N_SEQ * MOST
    slot = jnp.where(ids < EXPERTS_WIN, ids * (N_SEQ * MOST) + block * MOST + rank, dead)
    route = block * (TOK * TOPK) + jnp.arange(TOK * TOPK, dtype=jnp.int32)[None, :]
    table = jnp.full((dead + 1,), -1, jnp.int32).at[slot.reshape(-1)].set(route.reshape(-1).astype(jnp.int32))
    return table[:dead].reshape(EXPERTS_WIN, N_SEQ * MOST)


def reference(tokens, out_grad, expert_ids, gates, w_gate, w_up, w_down, shared_gate, shared_up, shared_down):
    table = route_table(expert_ids)
    flat_gates = gates.reshape(-1)
    dead = TOKENS * TOPK

    def expert_step(carry, inputs):
        grad_rows, grad_routes = carry
        weight_g, weight_u, weight_d, route = inputs
        used = route >= 0
        safe = jnp.where(used, route, 0).astype(jnp.int32)
        token_of = (safe // TOPK).astype(jnp.int32)
        rows_x = jnp.where(used[:, None], tokens[token_of], jnp.zeros((), jnp.bfloat16))
        rows_dy = jnp.where(used[:, None], out_grad[token_of], jnp.zeros((), jnp.bfloat16))
        weight = jnp.where(used, flat_gates[safe].astype(jnp.float32), jnp.float32(0.0))[:, None]
        pre_a = dot_last(rows_x, weight_g)
        pre_b = dot_last(rows_x, weight_u)
        act, slope = silu_parts(pre_a)
        hidden = act * pre_b
        back = dot_last(rows_dy, weight_d)
        dgate = jnp.sum(hidden * back, axis=1)
        scaled = weight * back
        grad_a = (scaled * pre_b * slope).astype(jnp.bfloat16)
        grad_b = (scaled * act).astype(jnp.bfloat16)
        hidden_w = (weight * hidden).astype(jnp.bfloat16)
        out_d = dot_rows(hidden_w, rows_dy).astype(jnp.bfloat16)
        out_g = dot_rows(grad_a, rows_x).astype(jnp.bfloat16)
        out_u = dot_rows(grad_b, rows_x).astype(jnp.bfloat16)
        part = group_sum(grad_a, grad_b, weight_g, weight_u)
        grad_rows = grad_rows.at[jnp.where(used, token_of, TOKENS)].add(part)
        grad_routes = grad_routes.at[jnp.where(used, safe, dead)].add(dgate)
        return (grad_rows, grad_routes), (out_g, out_u, out_d)

    start = (jnp.zeros((TOKENS + 1, D), jnp.float32), jnp.zeros((dead + 1,), jnp.float32))
    (grad_rows, grad_routes), (grad_gate, grad_up, grad_down) = lax.scan(expert_step, start, (w_gate, w_up, w_down, table))

    shared_gate_t = shared_gate.T
    shared_up_t = shared_up.T

    def shared_step(carry, inputs):
        block_x, block_dy = inputs
        pre_a = jnp.dot(block_x, shared_gate, preferred_element_type=jnp.float32)
        pre_b = jnp.dot(block_x, shared_up, preferred_element_type=jnp.float32)
        act, slope = silu_parts(pre_a)
        back = dot_last(block_dy, shared_down)
        grad_a = (back * pre_b * slope).astype(jnp.bfloat16)
        grad_b = (back * act).astype(jnp.bfloat16)
        hidden = (act * pre_b).astype(jnp.bfloat16)
        part_g = dot_rows(block_x, grad_a).astype(jnp.bfloat16).astype(jnp.float32)
        part_u = dot_rows(block_x, grad_b).astype(jnp.bfloat16).astype(jnp.float32)
        part_d = dot_rows(hidden, block_dy).astype(jnp.bfloat16).astype(jnp.float32)
        rows = group_sum(grad_a, grad_b, shared_gate_t, shared_up_t)
        return (carry[0] + part_g, carry[1] + part_u, carry[2] + part_d), rows

    zero_in = jnp.zeros((D, FS), jnp.float32)
    zero_out = jnp.zeros((FS, D), jnp.float32)
    blocks = (tokens.reshape(N_SEQ, TOK, D), out_grad.reshape(N_SEQ, TOK, D))
    (sum_g, sum_u, sum_d), shared_rows = lax.scan(shared_step, (zero_in, zero_in, zero_out), blocks)
    token_grad = (grad_rows[:TOKENS] + shared_rows.reshape(TOKENS, D)).astype(jnp.bfloat16)
    gate_grad = grad_routes[:dead].reshape(TOKENS, TOPK)
    return (token_grad, gate_grad, grad_gate, grad_up, grad_down,
            sum_g.astype(jnp.bfloat16), sum_u.astype(jnp.bfloat16), sum_d.astype(jnp.bfloat16))
```

```python
import functools

import jax
import jax.numpy as jnp
from jax import lax
from jax.experimental import pallas as pl
from jax.experimental.pallas import tpu as pltpu
from jax.sharding import PartitionSpec as P

MESH = pl.DeviceIdType.MESH
MOST = 12
SLOT = 16
SIDE = 4
BLOCK = 128
MIB = 1 << 20
F32 = jnp.float32
BF16 = jnp.bfloat16


def dot(left, right):
    return jnp.dot(left, right, preferred_element_type=F32)


def dot_last(left, right):
    return lax.dot_general(left, right, (((1,), (1,)), ((), ())), preferred_element_type=F32)


def dot_rows(left, right):
    return lax.dot_general(left, right, (((0,), (0,)), ((), ())), preferred_element_type=F32)


def silu_parts(value):
    sig = jax.nn.sigmoid(value)
    return value * sig, sig * (1.0 + value * (1.0 - sig))


def ring(value, size):
    return lax.rem(value + size, size)


def place():
    seq, exp = lax.axis_index("seq"), lax.axis_index("exp")
    return (
        seq,
        exp,
        lax.div(seq, 2 * SIDE),
        lax.rem(lax.div(seq, 2), SIDE),
        lax.rem(seq, 2),
    )


def remote(src, dst, send_sem, recv_sem, device):
    return pltpu.make_async_remote_copy(
        src_ref=src,
        dst_ref=dst,
        send_sem=send_sem,
        recv_sem=recv_sem,
        device_id=device,
        device_id_type=MESH,
    )


def greet(barrier, device):
    pl.semaphore_signal(barrier, inc=1, device_id=device, device_id_type=MESH)


def has_step(step, way, sub):
    return step < 4 or way == sub


class ZRing:
    def __init__(self, own, bufs, seq, exp, send_sem, recv_sem):
        self.own, self.bufs, self.seq, self.exp = own, bufs, seq, exp
        self.send_sem, self.recv_sem = send_sem, recv_sem

    def copy(self, step, way, sub, landed=False):
        sign = 1 - 2 * way
        piece = ring(self.exp - sign * (step if landed else step - 1), 8)
        slot = self.bufs[sub].at[piece]
        src = self.own[sub] if step == 1 and not landed else slot
        return remote(
            src,
            slot,
            self.send_sem.at[way, sub, step - 1],
            self.recv_sem.at[way, sub, step - 1],
            (self.seq, ring(self.exp + sign, 8)),
        )

    def start(self, step):
        for sub in range(2):
            for way in range(2):
                if has_step(step, way, sub):
                    self.copy(step, way, sub).start()

    def land(self, step):
        for sub in range(2):
            for way in range(2):
                if has_step(step, way, sub):
                    self.copy(step, way, sub, landed=True).wait_recv()
                    if step < 4 and has_step(step + 1, way, sub):
                        self.copy(step + 1, way, sub).start()

    def finish(self):
        for step in range(1, 5):
            for sub in range(2):
                for way in range(2):
                    if has_step(step, way, sub):
                        self.copy(step, way, sub).wait_send()


class Plane:
    def __init__(self):
        self.seq, self.exp, self.x, self.y, self.core = place()

    def device(self, along_x, step):
        x = ring(self.x + step, SIDE) if along_x else self.x
        y = self.y if along_x else ring(self.y + step, SIDE)
        return ((x * SIDE + y) * 2 + self.core, self.exp)

    def view(self, ref, half, wide, along_x, step):
        count = ref.shape[3] // 2
        rows = pl.ds(half * count, count)
        here = ring((self.x if along_x else self.y) + step, SIDE)
        if along_x:
            return ref.at[here, :, self.core, rows] if wide else ref.at[here, self.y, self.core, rows]
        return ref.at[:, here, self.core, rows] if wide else ref.at[self.x, here, self.core, rows]


def spread_kernel(
    send, tok, grad, shared, rows_o, tok_o, grad_o, shared_o, own_sem, a_s, a_r, z_s, z_r, w_s, w_r, b_s, b_r
):
    plane = Plane()
    seq, exp, core = plane.seq, plane.exp, plane.core
    sibling = (seq + 1 - 2 * core, exp)
    own = [
        pltpu.make_async_copy(send.at[seq], rows_o.at[seq], own_sem.at[0]),
        pltpu.make_async_copy(tok, tok_o.at[exp], own_sem.at[1]),
        pltpu.make_async_copy(grad, grad_o.at[exp], own_sem.at[2]),
        pltpu.make_async_copy(shared, shared_o.at[plane.x, plane.y, core], own_sem.at[3]),
    ]
    for copy in own:
        copy.start()
    barrier = pltpu.get_barrier_semaphore()

    def hello(step, carry):
        greet(barrier, (ring(seq + step, 32), exp))
        return carry

    lax.fori_loop(1, 32, hello, 0)
    greet(barrier, (seq, ring(exp + 1, 8)))
    greet(barrier, (seq, ring(exp - 1, 8)))
    pl.semaphore_wait(barrier, 33)

    tokens = ZRing((tok, grad), (tok_o, grad_o), seq, exp, z_s, z_r)
    tokens.start(1)

    def exchange(step, landed):
        to, source = ring(seq + step, 32), ring(seq - step, 32)
        return remote(
            send.at[to],
            rows_o.at[source if landed else seq],
            a_s.at[step - 1],
            a_r.at[step - 1],
            (to, exp),
        )

    def exchange_start(step, carry):
        exchange(step, False).start()
        return carry

    lax.fori_loop(1, 32, exchange_start, 0)
    own[3].wait()

    def weight(half, phase, kind, landed):
        along_x = half != phase
        sign = 1 - 2 * half
        wide = phase == 1
        if kind == 0:
            to, piece = sign, (-sign if landed else 0)
        elif kind == 1:
            to, piece = -sign, (sign if landed else 0)
        else:
            to, piece = sign, (2 if landed else -sign)
        part = plane.view(shared_o, half, wide, along_x, piece)
        return remote(
            part, part, w_s.at[half, phase, kind], w_r.at[half, phase, kind], plane.device(along_x, to)
        )

    def across(half, phase, index, landed):
        along_x = half != phase
        sign = 1 - 2 * half
        wide = phase == 1
        piece = (0, -sign, sign, 2)[index]
        core_here = plane.core
        if landed:
            plane.core = 1 - core_here
        part = plane.view(shared_o, half, wide, along_x, piece)
        plane.core = core_here
        return remote(part, part, b_s.at[half, phase, index], b_r.at[half, phase, index], sibling)

    for half in range(2):
        weight(half, 0, 0, False).start()
        weight(half, 0, 1, False).start()
        across(half, 0, 0, False).start()

    def weight_near(phase):
        for half in range(2):
            weight(half, phase, 0, True).wait_recv()
            weight(half, phase, 2, False).start()
            across(half, phase, 1, False).start()
            weight(half, phase, 1, True).wait_recv()
            across(half, phase, 2, False).start()

    def weight_far(phase):
        for half in range(2):
            weight(half, phase, 2, True).wait_recv()
            if phase == 0:
                weight(half, 1, 0, False).start()
                weight(half, 1, 1, False).start()
            across(half, phase, 3, False).start()

    weight_near(0)
    weight_far(0)
    tokens.land(1)
    weight_near(1)
    tokens.land(2)
    weight_far(1)
    tokens.land(3)
    tokens.land(4)

    def exchange_end(step, carry):
        exchange(step, True).wait_recv()
        exchange(step, False).wait_send()
        return carry

    lax.fori_loop(1, 32, exchange_end, 0)
    for copy in own[:3]:
        copy.wait()
    tokens.finish()
    for half in range(2):
        for phase in range(2):
            for kind in range(3):
                weight(half, phase, kind, False).wait_send()
            for index in range(1 if phase else 0, 4):
                across(half, phase, index, True).wait_recv()
                across(half, phase, index, False).wait_send()


def any_specs(count):
    return [pl.BlockSpec(memory_space=pl.ANY)] * count


def vmem_specs(count):
    return [pl.BlockSpec(memory_space=pltpu.VMEM)] * count


def spread(send, tok, grad, shared):
    rows, width = tok.shape
    dma = pltpu.SemaphoreType.DMA
    return pl.pallas_call(
        spread_kernel,
        out_shape=(
            jax.ShapeDtypeStruct(send.shape, BF16),
            jax.ShapeDtypeStruct((8, rows, width), BF16),
            jax.ShapeDtypeStruct((8, rows, width), BF16),
            jax.ShapeDtypeStruct((SIDE, SIDE, 2) + shared.shape, BF16),
        ),
        in_specs=any_specs(4),
        out_specs=any_specs(4),
        scratch_shapes=[
            dma((4,)),
            dma((31,)),
            dma((31,)),
            dma((2, 2, 4)),
            dma((2, 2, 4)),
            dma((2, 2, 3)),
            dma((2, 2, 3)),
            dma((2, 2, 4)),
            dma((2, 2, 4)),
        ],
        compiler_params=pltpu.CompilerParams(collective_id=0, has_side_effects=True),
    )(send, tok, grad, shared)


def back_kernel(send, rows_o, own_sem, a_s, a_r):
    seq, exp = lax.axis_index("seq"), lax.axis_index("exp")
    own = pltpu.make_async_copy(send.at[seq], rows_o.at[seq], own_sem)
    own.start()
    barrier = pltpu.get_barrier_semaphore()

    def hello(step, carry):
        greet(barrier, (ring(seq + step, 32), exp))
        return carry

    lax.fori_loop(1, 32, hello, 0)
    pl.semaphore_wait(barrier, 31)

    def exchange(step, landed):
        to, source = ring(seq + step, 32), ring(seq - step, 32)
        return remote(
            send.at[to],
            rows_o.at[source if landed else seq],
            a_s.at[step - 1],
            a_r.at[step - 1],
            (to, exp),
        )

    def exchange_start(step, carry):
        exchange(step, False).start()
        return carry

    def exchange_end(step, carry):
        exchange(step, True).wait_recv()
        exchange(step, False).wait_send()
        return carry

    lax.fori_loop(1, 32, exchange_start, 0)
    lax.fori_loop(1, 32, exchange_end, 0)
    own.wait()


def send_back(send):
    dma = pltpu.SemaphoreType.DMA
    return pl.pallas_call(
        back_kernel,
        out_shape=jax.ShapeDtypeStruct(send.shape, BF16),
        in_specs=vmem_specs(1),
        out_specs=vmem_specs(1)[0],
        scratch_shapes=[dma, dma((31,)), dma((31,))],
        compiler_params=pltpu.CompilerParams(collective_id=3, has_side_effects=True),
    )(send)


def expert_kernel(
    row_x, row_y, gate, w_gate, w_up, w_down, tok, grad, shared,
    row_sum, shared_rows, out_gate, out_up, out_down, out_shared,
    xb, yb, wg, wu, wd, tx, ty, ws,
    s_acc, s_dab, s_h, gp, sib, qa, qb,
    acc_a, acc_b, acc_u, da, db, hw, dat, dbt, hwt, dg,
    pb, rp, rm, stage,
    own_sem, z_s, z_r, c_s, c_r, q_s, q_r, p_s, p_r, o_s,
):
    plane = Plane()
    seq, exp, core = plane.seq, plane.exp, plane.core
    sibling = (seq + 1 - 2 * core, exp)
    count, width = row_x.shape
    tok_rows = tok.shape[1]
    total = count + 16 + tok_rows
    split = -(-total // 32) * 16
    lanes = ws.shape[2] // 3

    own = [
        pltpu.make_async_copy(src, dst, own_sem.at[i])
        for i, (src, dst) in enumerate(
            (
                (tok, tx),
                (grad, ty),
                (shared, ws),
                (row_x, xb.at[exp]),
                (row_y, yb.at[exp]),
                (w_gate, wg),
                (w_up, wu),
                (w_down, wd),
            )
        )
    ]
    for copy in own:
        copy.start()
    barrier = pltpu.get_barrier_semaphore()
    greet(barrier, (seq, ring(exp + 1, 8)))
    greet(barrier, (seq, ring(exp - 1, 8)))
    greet(barrier, plane.device(True, 1))
    greet(barrier, plane.device(True, -1))
    greet(barrier, plane.device(False, 1))
    greet(barrier, plane.device(False, -1))
    greet(barrier, sibling)
    pl.semaphore_wait(barrier, 7)

    rows = ZRing((row_x, row_y), (xb, yb), seq, exp, z_s, z_r)
    rows.start(1)

    for copy in own[:3]:
        copy.wait()
    s_acc[...] = jnp.zeros_like(s_acc)

    def shared_forward(piece, carry):
        s_acc[:, : 2 * lanes] += dot(tx[piece], ws[piece, :, : 2 * lanes])
        s_acc[:, 2 * lanes :] += dot(ty[piece], ws[piece, :, 2 * lanes :])
        return carry

    lax.fori_loop(0, 8, shared_forward, 0)
    act, slope = silu_parts(s_acc[:, :lanes])
    up, back = s_acc[:, lanes : 2 * lanes], s_acc[:, 2 * lanes :]
    s_dab[:, :lanes] = (back * up * slope).astype(BF16)
    s_dab[:, lanes:] = (back * act).astype(BF16)
    s_h[...] = (act * up).astype(BF16)

    def shared_grads(piece, carry):
        at_x, at_y = lax.div(piece, 2), 2 * lax.rem(piece, 2)
        part = dot_rows(tx[piece], s_dab[...]).astype(BF16)
        gp[at_x, pl.ds(at_y, 2), :, :, : 2 * lanes] = part.reshape(2, 2, width // 4, 2 * lanes)
        part = dot_rows(ty[piece], s_h[...]).astype(BF16)
        gp[at_x, pl.ds(at_y, 2), :, :, 2 * lanes :] = part.reshape(2, 2, width // 4, lanes)
        return carry

    lax.fori_loop(0, 8, shared_grads, 0)
    across = remote(gp.at[:, :, 1 - core], sib, c_s, c_r, sibling)
    across.start()

    for copy in own[3:]:
        copy.wait()
    acc_a[...] = jnp.zeros_like(acc_a)
    acc_b[...] = jnp.zeros_like(acc_b)
    acc_u[...] = jnp.zeros_like(acc_u)

    def forward(piece):
        cols = pl.ds(pl.multiple_of(piece * width, 128), width)

        def block(index, carry):
            at = pl.ds(pl.multiple_of(index * BLOCK, BLOCK), BLOCK)
            acc_a[at] += dot_last(xb[piece, at], wg[:, cols])
            acc_b[at] += dot_last(xb[piece, at], wu[:, cols])
            acc_u[at] += dot_last(yb[piece, at], wd[:, cols])
            return carry

        lax.fori_loop(0, count // BLOCK, block, 0)

    forward(exp)

    def landing(half, phase, kind):
        return qb.at[half, kind] if phase else qa.at[half, kind]

    def reduce_copy(half, phase, kind):
        along_x = half == phase
        sign = 1 - 2 * half
        piece, to = ((2, sign), (-sign, -sign), (sign, sign))[kind]
        return remote(
            plane.view(gp, half, phase == 0, along_x, piece),
            landing(half, phase, kind),
            q_s.at[half, phase, kind],
            q_r.at[half, phase, kind],
            plane.device(along_x, to),
        )

    def reduce_add(half, phase, step, kinds):
        mine = plane.view(gp, half, phase == 0, half == phase, step)
        value = mine[...].astype(F32)
        for kind in kinds:
            value += landing(half, phase, kind)[...].astype(F32)
        mine[...] = value.astype(BF16)

    def reduce_start(phase):
        for half in range(2):
            reduce_copy(half, phase, 0).start()
            reduce_copy(half, phase, 1).start()

    def reduce_pass(phase):
        for half in range(2):
            reduce_copy(half, phase, 0).wait_recv()
            reduce_add(half, phase, 1 - 2 * half, (0,))
            reduce_copy(half, phase, 2).start()

    def reduce_end(phase):
        for half in range(2):
            reduce_copy(half, phase, 1).wait_recv()
            reduce_copy(half, phase, 2).wait_recv()
            reduce_add(half, phase, 0, (1, 2))

    across.wait_recv()

    def add_sibling(index, carry):
        at_x, at_y = lax.div(index, SIDE), lax.rem(index, SIDE)
        gp[at_x, at_y, core] = (
            gp[at_x, at_y, core].astype(F32) + sib[at_x, at_y].astype(F32)
        ).astype(BF16)
        return carry

    lax.fori_loop(0, SIDE * SIDE, add_sibling, 0)
    reduce_start(0)

    rows.land(1)
    forward(ring(exp - 1, 8))
    forward(ring(exp + 1, 8))
    reduce_pass(0)
    rows.land(2)
    forward(ring(exp - 2, 8))
    forward(ring(exp + 2, 8))
    reduce_end(0)
    reduce_start(1)
    rows.land(3)
    forward(ring(exp - 3, 8))
    forward(ring(exp + 3, 8))
    reduce_pass(1)
    rows.land(4)
    forward(ring(exp + 4, 8))

    dg[...] = jnp.zeros_like(dg)
    for index in range(count // BLOCK):
        at = pl.ds(index * BLOCK, BLOCK)
        act, slope = silu_parts(acc_a[at])
        up, back = acc_b[at], acc_u[at]
        hidden = act * up
        dg[:, at] = lax.dot_general(
            jnp.ones((16, hidden.shape[1]), F32),
            hidden * back,
            (((1,), (1,)), ((), ())),
            preferred_element_type=F32,
            precision=lax.Precision.HIGHEST,
        ).astype(BF16)
        scaled = gate[at] * back
        grad_a = (scaled * up * slope).astype(BF16)
        grad_b = (scaled * act).astype(BF16)
        hidden_w = (gate[at] * hidden).astype(BF16)
        da[at], db[at], hw[at] = grad_a, grad_b, hidden_w
        dat[:, at], dbt[:, at], hwt[:, at] = grad_a.T, grad_b.T, hidden_w.T

    def partial(piece):
        cols = pl.ds(pl.multiple_of(piece * width, 128), width)

        def block(index, carry):
            at = pl.ds(pl.multiple_of(index * BLOCK, BLOCK), BLOCK)
            pb[piece, at] = (dot(da[at], wg[:, cols]) + dot(db[at], wu[:, cols])).astype(BF16)
            return carry

        lax.fori_loop(0, count // BLOCK, block, 0)
        pb[piece, count : count + 16] = dg[...]
        pb[piece, count + 16 :] = dot_last(s_dab[...], ws[piece, :, : 2 * lanes]).astype(BF16)

    parts = (pl.ds(0, split), pl.ds(split, total - split))
    landed = (rp, rm)

    def sum_copy(step, way, sub):
        sign = 1 - 2 * way
        return remote(
            pb.at[ring(exp + sign * (5 - step), 8), parts[sub]],
            landed[way].at[step - 1, parts[sub]],
            p_s.at[way, sub, step - 1],
            p_r.at[way, sub, step - 1],
            (seq, ring(exp + sign, 8)),
        )

    def has_sum(step, way, sub):
        return step > 1 or way == sub

    def sum_step(step):
        for sub in range(2):
            for way in range(2):
                if has_sum(step - 1, way, sub):
                    sum_copy(step - 1, way, sub).wait_recv()
                    piece = ring(exp + (1 - 2 * way) * (5 - step), 8)
                    pb[piece, parts[sub]] = (
                        pb[piece, parts[sub]].astype(F32)
                        + landed[way][step - 2, parts[sub]].astype(F32)
                    ).astype(BF16)
                sum_copy(step, way, sub).start()

    outs = (out_gate, out_up, out_down)

    def out_copy(index, which):
        piece = ring(exp + index, 8)
        cols = pl.ds(pl.multiple_of(piece * width, 128), width)
        return pltpu.make_async_copy(
            stage.at[index % 2, which], outs[which].at[:, cols], o_s.at[index % 2, which]
        )

    def weight_grads(index):
        piece = ring(exp + index, 8)
        if index >= 2:
            for which in range(3):
                out_copy(index - 2, which).wait()
        stage[index % 2, 0] = dot(dat[...], xb[piece]).astype(BF16)
        stage[index % 2, 1] = dot(dbt[...], xb[piece]).astype(BF16)
        stage[index % 2, 2] = dot(hwt[...], yb[piece]).astype(BF16)
        for which in range(3):
            out_copy(index, which).start()

    partial(ring(exp + 4, 8))
    sum_copy(1, 0, 0).start()
    sum_copy(1, 1, 1).start()
    partial(ring(exp + 3, 8))
    partial(ring(exp - 3, 8))
    sum_step(2)
    partial(ring(exp + 2, 8))
    partial(ring(exp - 2, 8))
    reduce_end(1)
    out_shared[...] = gp[plane.x, plane.y, core]
    weight_grads(0)
    weight_grads(1)
    sum_step(3)
    partial(ring(exp + 1, 8))
    partial(ring(exp - 1, 8))
    weight_grads(2)
    weight_grads(3)
    sum_step(4)
    partial(exp)
    for index in range(4, 8):
        weight_grads(index)
    for sub in range(2):
        for way in range(2):
            sum_copy(4, way, sub).wait_recv()
    whole = pb[exp].astype(F32) + rp[3].astype(F32) + rm[3].astype(F32)
    row_sum[...] = whole[: count + 16].astype(BF16)
    shared_rows[...] = whole[count + 16 :]

    rows.finish()
    across.wait_send()
    for half in range(2):
        for phase in range(2):
            for kind in range(3):
                reduce_copy(half, phase, kind).wait_send()
    for step in range(1, 5):
        for way in range(2):
            for sub in range(2):
                if has_sum(step, way, sub):
                    sum_copy(step, way, sub).wait_send()
    for index in (6, 7):
        for which in range(3):
            out_copy(index, which).wait()


def expert(row_x, row_y, gate, w_gate, w_up, w_down, tok, grad, shared, collective_id):
    count, width = row_x.shape
    hidden, model = w_gate.shape
    tok_rows = tok.shape[1]
    total = count + 16 + tok_rows
    chunk, lanes = shared.shape[3:]
    dma = pltpu.SemaphoreType.DMA
    vmem = pltpu.VMEM
    routed = jax.ShapeDtypeStruct((hidden, model), BF16)
    return pl.pallas_call(
        expert_kernel,
        out_shape=(
            jax.ShapeDtypeStruct((count + 16, width), BF16),
            jax.ShapeDtypeStruct((tok_rows, width), F32),
            routed,
            routed,
            routed,
            jax.ShapeDtypeStruct((chunk, lanes), BF16),
        ),
        in_specs=any_specs(2) + vmem_specs(1) + any_specs(6),
        out_specs=vmem_specs(2) + any_specs(3) + vmem_specs(1),
        scratch_shapes=[
            vmem((8, count, width), BF16),
            vmem((8, count, width), BF16),
            vmem((hidden, model), BF16),
            vmem((hidden, model), BF16),
            vmem((hidden, model), BF16),
            vmem((8, tok_rows, width), BF16),
            vmem((8, tok_rows, width), BF16),
            vmem((8, width, lanes), BF16),
            vmem((tok_rows, lanes), F32),
            vmem((tok_rows, lanes // 3 * 2), BF16),
            vmem((tok_rows, lanes // 3), BF16),
            vmem((SIDE, SIDE, 2, chunk, lanes), BF16),
            vmem((SIDE, SIDE, chunk, lanes), BF16),
            vmem((2, 3, SIDE, chunk // 2, lanes), BF16),
            vmem((2, 3, chunk // 2, lanes), BF16),
            vmem((count, hidden), F32),
            vmem((count, hidden), F32),
            vmem((count, hidden), F32),
            vmem((count, hidden), BF16),
            vmem((count, hidden), BF16),
            vmem((count, hidden), BF16),
            vmem((hidden, count), BF16),
            vmem((hidden, count), BF16),
            vmem((hidden, count), BF16),
            vmem((16, width), BF16),
            vmem((8, total, width), BF16),
            vmem((4, total, width), BF16),
            vmem((4, total, width), BF16),
            vmem((2, 3, hidden, width), BF16),
            dma((8,)),
            dma((2, 2, 4)),
            dma((2, 2, 4)),
            dma,
            dma,
            dma((2, 2, 3)),
            dma((2, 2, 3)),
            dma((2, 2, 4)),
            dma((2, 2, 4)),
            dma((2, 3)),
        ],
        compiler_params=pltpu.CompilerParams(
            collective_id=collective_id, has_side_effects=True, vmem_limit_bytes=62 * MIB
        ),
    )(row_x, row_y, gate, w_gate, w_up, w_down, tok, grad, shared.reshape(8, width, lanes))


def with_side(rows, side, at):
    wide = jnp.pad(side, ((0, 0), (0, rows.shape[2] - side.shape[1])))
    row = lax.broadcasted_iota(jnp.int32, rows.shape, 1)
    return jnp.where(row == at, wide[:, None, :].astype(rows.dtype), rows)


def body(
    tokens, out_grad, expert_ids, gates, w_gate, w_up, w_down, shared_gate, shared_up, shared_down
):
    tok_rows, width = tokens.shape
    experts = 32
    window = jnp.arange(experts, dtype=jnp.int32)
    onehot = (expert_ids[:, :, None] == window).astype(F32)
    named = jnp.sum(onehot, axis=1)
    gate_of = jnp.sum(onehot * gates.astype(F32)[:, :, None], axis=1)
    order = jnp.arange(tok_rows, dtype=jnp.int32)
    earlier = (order[None, :] < order[:, None]).astype(BF16)
    rank = dot(earlier, named.astype(BF16))
    rank = jnp.where(named > 0, rank, -1.0)
    slots = jnp.arange(SLOT, dtype=jnp.int32).astype(F32)
    pick = (rank.T[:, None, :] == slots[None, :, None]).astype(F32)
    pick_flat = pick.astype(BF16).reshape(experts * SLOT, tok_rows)
    slot_gate = jnp.sum(pick * gate_of.T[:, None, :], axis=2)
    counts = jnp.broadcast_to(jnp.sum(named, axis=0)[None, :], (experts, experts))
    both = jnp.concatenate([tokens, out_grad], axis=1)
    send = dot(pick_flat, both).astype(BF16).reshape(experts, SLOT, 2 * width)
    send = with_side(with_side(send, slot_gate, MOST), counts, MOST + 1)

    def widen(part):
        return jnp.pad(part, ((0, 0), (0, 256 - part.shape[1])))

    shared = jnp.concatenate([widen(shared_gate), widen(shared_up), widen(shared_down.T)], axis=1)
    got, full_x, full_y, whole = spread(send, tokens, out_grad, shared)

    counts = got[:, MOST + 1, :experts].astype(F32)
    per_expert = jnp.sum(counts, axis=0)
    here = lax.axis_index("seq")
    mine = jnp.sum(jnp.where(window[None, :] == here, counts, 0.0), axis=1)
    first = jnp.sum(jnp.where(window[None, :] < window[:, None], mine[None, :], 0.0), axis=1)
    spot = jnp.where(slots[None, :] < mine[:, None], first[:, None] + slots[None, :], -1.0)
    got_gate = got[:, MOST, :SLOT].reshape(1, experts * SLOT).astype(F32)
    got_flat = got.reshape(experts * SLOT, 2 * width)

    def run(count, collective_id):
        index = jnp.arange(count, dtype=jnp.int32).astype(F32)
        pack = (spot.reshape(1, experts * SLOT) == index[:, None]).astype(F32)
        row_gate = jnp.sum(pack * got_gate, axis=1, keepdims=True)
        pack = pack.astype(BF16)
        row_x = dot(pack, got_flat[:, :width]).astype(BF16)
        row_y = dot(pack, got_flat[:, width:]).astype(BF16)
        row_sum, shared_rows, grad_gate, grad_up, grad_down, grad_shared = expert(
            row_x, row_y, row_gate, w_gate[0], w_up[0], w_down[0], full_x, full_y, whole, collective_id
        )
        rows = dot_rows(pack, row_sum[:count]).astype(BF16).reshape(experts, SLOT, width)
        route = jnp.sum(pack.astype(F32) * row_sum[count, :count].astype(F32)[:, None], axis=0)
        rows = with_side(rows, route.reshape(experts, SLOT), MOST)
        return rows, shared_rows, grad_gate, grad_up, grad_down, grad_shared

    rows, shared_rows, grad_gate, grad_up, grad_down, grad_shared = run(experts * MOST, 2)
    back = send_back(rows)
    routed = dot_rows(pick_flat, back.reshape(experts * SLOT, width))
    token_grad = (routed + shared_rows).astype(BF16)
    route = jnp.sum(pick * back[:, MOST, :SLOT].astype(F32)[:, :, None], axis=1)
    gate_grad = jnp.sum(onehot * route.T[:, None, :], axis=2)
    hidden = shared_gate.shape[1]
    return (
        token_grad,
        gate_grad,
        grad_gate[None],
        grad_up[None],
        grad_down[None],
        grad_shared[:, :hidden],
        grad_shared[:, 256 : 256 + hidden],
        grad_shared[:, 512 : 512 + hidden].T,
    )


def solution(mesh):
    return jax.shard_map(
        body,
        mesh=mesh,
        in_specs=(
            P("seq", "exp"),
            P("seq", "exp"),
            P("seq", None),
            P("seq", None),
            P("seq", "exp", None),
            P("seq", "exp", None),
            P("seq", "exp", None),
            P("seq", "exp"),
            P("seq", "exp"),
            P("exp", "seq"),
        ),
        out_specs=(
            P("seq", "exp"),
            P("seq", None),
            P("seq", "exp", None),
            P("seq", "exp", None),
            P("seq", "exp", None),
            P("seq", "exp"),
            P("seq", "exp"),
            P("exp", "seq"),
        ),
        check_vma=False,
    )
```

```python
import functools

import jax
import jax.numpy as jnp
from jax import lax
from jax.experimental import pallas as pl
from jax.experimental.pallas import tpu as pltpu
from jax.sharding import PartitionSpec as P

MESH = pl.DeviceIdType.MESH
MOST = 12
SLOT = 16
SIDE = 4
BLOCK = 128
FAR = 1
MIB = 1 << 20
F32 = jnp.float32
BF16 = jnp.bfloat16


def dot(left, right):
    return jnp.dot(left, right, preferred_element_type=F32)


def dot_last(left, right):
    return lax.dot_general(left, right, (((1,), (1,)), ((), ())), preferred_element_type=F32)


def dot_rows(left, right):
    return lax.dot_general(left, right, (((0,), (0,)), ((), ())), preferred_element_type=F32)


def silu_parts(value):
    sig = jax.nn.sigmoid(value)
    return value * sig, sig * (1.0 + value * (1.0 - sig))


def ring(value, size):
    return lax.rem(value + size, size)


def place():
    seq, exp = lax.axis_index("seq"), lax.axis_index("exp")
    return (
        seq,
        exp,
        lax.div(seq, 2 * SIDE),
        lax.rem(lax.div(seq, 2), SIDE),
        lax.rem(seq, 2),
    )


def remote(src, dst, send_sem, recv_sem, device):
    return pltpu.make_async_remote_copy(
        src_ref=src,
        dst_ref=dst,
        send_sem=send_sem,
        recv_sem=recv_sem,
        device_id=device,
        device_id_type=MESH,
    )


def greet(barrier, device):
    pl.semaphore_signal(barrier, inc=1, device_id=device, device_id_type=MESH)


class ZRing:
    def __init__(self, own, bufs, seq, exp, send_sem, recv_sem, full=3, half=True):
        self.own, self.bufs, self.seq, self.exp = own, bufs, seq, exp
        self.send_sem, self.recv_sem = send_sem, recv_sem
        self.full, self.half = full, half

    def has(self, step, way, sub):
        return step <= self.full or (self.half and step == self.full + 1 and way == sub)

    def copy(self, step, way, sub, landed=False):
        sign = 1 - 2 * way
        piece = ring(self.exp - sign * (step if landed else step - 1), 8)
        slot = self.bufs[sub].at[piece]
        src = self.own[sub] if step == 1 and not landed else slot
        return remote(
            src,
            slot,
            self.send_sem.at[way, sub, step - 1],
            self.recv_sem.at[way, sub, step - 1],
            (self.seq, ring(self.exp + sign, 8)),
        )

    def start(self, step):
        for sub in range(2):
            for way in range(2):
                if self.has(step, way, sub):
                    self.copy(step, way, sub).start()

    def land(self, step):
        for sub in range(2):
            for way in range(2):
                if self.has(step, way, sub):
                    self.copy(step, way, sub, landed=True).wait_recv()
                    if self.has(step + 1, way, sub):
                        self.copy(step + 1, way, sub).start()

    def finish(self):
        for step in range(1, 5):
            for sub in range(2):
                for way in range(2):
                    if self.has(step, way, sub):
                        self.copy(step, way, sub).wait_send()


class ZSum:
    def __init__(self, own, landed, split, seq, exp, send_sem, recv_sem):
        self.own, self.landed, self.seq, self.exp = own, landed, seq, exp
        self.send_sem, self.recv_sem = send_sem, recv_sem
        self.parts = (pl.ds(0, split), pl.ds(split, own.shape[1] - split))

    def has(self, step, way, sub):
        return step > 1 or way == sub

    def copy(self, step, way, sub):
        sign = 1 - 2 * way
        return remote(
            self.own.at[ring(self.exp + sign * (5 - step), 8), self.parts[sub]],
            self.landed[way].at[step - 1, self.parts[sub]],
            self.send_sem.at[way, sub, step - 1],
            self.recv_sem.at[way, sub, step - 1],
            (self.seq, ring(self.exp + sign, 8)),
        )

    def step(self, step):
        for sub in range(2):
            for way in range(2):
                if step > 1 and self.has(step - 1, way, sub):
                    self.copy(step - 1, way, sub).wait_recv()
                    piece = ring(self.exp + (1 - 2 * way) * (5 - step), 8)
                    part = self.parts[sub]
                    self.own[piece, part] = (
                        self.own[piece, part].astype(F32) + self.landed[way][step - 2, part].astype(F32)
                    ).astype(BF16)
                if self.has(step, way, sub):
                    self.copy(step, way, sub).start()

    def total(self):
        for sub in range(2):
            for way in range(2):
                self.copy(4, way, sub).wait_recv()
        return sum(part.astype(F32) for part in (self.own[self.exp], self.landed[0][3], self.landed[1][3]))

    def finish(self):
        for step in range(1, 5):
            for way in range(2):
                for sub in range(2):
                    if self.has(step, way, sub):
                        self.copy(step, way, sub).wait_send()


class Plane:
    def __init__(self):
        self.seq, self.exp, self.x, self.y, self.core = place()

    def device(self, along_x, step):
        x = ring(self.x + step, SIDE) if along_x else self.x
        y = self.y if along_x else ring(self.y + step, SIDE)
        return ((x * SIDE + y) * 2 + self.core, self.exp)

    def view(self, ref, half, wide, along_x, step):
        count = ref.shape[3] // 2
        rows = pl.ds(half * count, count)
        here = ring((self.x if along_x else self.y) + step, SIDE)
        if along_x:
            return ref.at[here, :, self.core, rows] if wide else ref.at[here, self.y, self.core, rows]
        return ref.at[:, here, self.core, rows] if wide else ref.at[self.x, here, self.core, rows]


def one_hot(rows, columns, shift):
    row = lax.broadcasted_iota(jnp.int32, (rows, columns), 0)
    column = lax.broadcasted_iota(jnp.int32, (rows, columns), 1)
    return jnp.where(row == column + shift, 1.0, 0.0).astype(BF16)


def half_lanes(rows, high):
    lane = lax.broadcasted_iota(jnp.int32, (rows, 128), 1)
    return jnp.where((lane >= 64) == high, 1.0, 0.0).astype(BF16)


def layer_kernel(
    ids, gates, tok, grad, w_gate, w_up, w_down, shared_gate, shared_up, shared_down,
    out_tok, out_route, out_gate, out_up, out_down, out_shared,
    pick, send, got, far_send, far_got, pack, gate, xb, yb, wg, wu, wd, tx, ty, ws,
    s_acc, s_dab, s_h, gp, sib, qa, qb,
    acc_a, acc_b, acc_u, da, db, hw, dat, dbt, hwt, dg,
    pb, rp, rm, sb, sp, sm, stage, send_b, got_b,
    own_sem, a_s, a_r, f_s, f_r, t_s, t_r, w_s, w_r, b_s, b_r, z_s, z_r, c_s, c_r, q_s, q_r,
    p_s, p_r, g_s, g_r, o_s, e_s, e_r,
):
    plane = Plane()
    seq, exp, core = plane.seq, plane.exp, plane.core
    sibling = (seq + 1 - 2 * core, exp)
    count = pack.shape[0]
    tok_rows, width = tok.shape
    slots = send.shape[0]
    of_x, lanes = s_dab.shape[1], ws.shape[4]

    own = [
        pltpu.make_async_copy(src, dst, own_sem.at[i])
        for i, (src, dst) in enumerate(
            ((tok, tx.at[exp]), (grad, ty.at[exp]), (w_gate, wg), (w_up, wu), (w_down, wd))
        )
    ]
    for copy in own:
        copy.start()

    barrier = pltpu.get_barrier_semaphore()

    def hello(step, carry):
        greet(barrier, (ring(seq + step, 32), exp))
        return carry

    lax.fori_loop(1, 32, hello, 0)
    greet(barrier, (seq, ring(exp + 1, 8)))
    greet(barrier, (seq, ring(exp - 1, 8)))

    experts = slots // SLOT
    expert = lax.broadcasted_iota(jnp.int32, (experts, tok_rows), 0)
    named = jnp.zeros((experts, tok_rows), F32)
    gate_of = jnp.zeros((experts, tok_rows), F32)
    for k in range(ids.shape[0]):
        hit = ids[k : k + 1] == expert
        named += jnp.where(hit, 1.0, 0.0)
        gate_of += jnp.where(hit, gates[k : k + 1].astype(F32), 0.0)
    row = lax.broadcasted_iota(jnp.int32, (tok_rows, tok_rows), 0)
    lane = lax.broadcasted_iota(jnp.int32, (tok_rows, tok_rows), 1)
    earlier = jnp.where(row < lane, 1.0, 0.0)
    rank = jnp.where(named > 0.0, dot(named.astype(BF16), earlier.astype(BF16)), -1.0)
    slot = lax.broadcasted_iota(jnp.int32, (slots, experts), 0)
    to_expert = lax.shift_right_logical(slot, 4) == lax.broadcasted_iota(jnp.int32, (slots, experts), 1)
    spread = jnp.where(to_expert, 1.0, 0.0).astype(BF16)
    slot = lax.broadcasted_iota(jnp.int32, (slots, tok_rows), 0)
    picked = dot(spread, rank.astype(BF16)) == lax.bitwise_and(slot, SLOT - 1).astype(F32)
    pick[...] = jnp.where(picked, 1.0, 0.0).astype(BF16)

    units = shared_gate.shape[1]
    ws[plane.x, plane.y, core, :, :128] = shared_gate[:, :128]
    ws[plane.x, plane.y, core, :, 128:256] = shared_up[:, :128]
    ws[plane.x, plane.y, core, :, 256:384] = (
        dot(shared_gate[...], one_hot(units, 128, 128)) + dot(shared_up[...], one_hot(units, 128, 64) * half_lanes(units, True))
    ).astype(BF16)
    ws[plane.x, plane.y, core, :, 384:512] = shared_down[:, :128]
    ws[plane.x, plane.y, core, :, 512:] = dot(shared_down[...], one_hot(units, 128, 128)).astype(BF16)
    pl.semaphore_wait(barrier, 33)

    tokens = ZRing((tok, grad), (tx, ty), seq, exp, t_s, t_r)
    tokens.start(1)

    def exchange(src, dst, s_sem, r_sem, step, landed):
        to, source = ring(seq + step, 32), ring(seq - step, 32)
        at = (source if landed else seq) * SLOT
        return remote(
            src.at[pl.ds(pl.multiple_of(to * SLOT, SLOT), SLOT)],
            dst.at[pl.ds(pl.multiple_of(at, SLOT), SLOT)],
            s_sem.at[step - 1],
            r_sem.at[step - 1],
            (to, exp),
        )

    def exchange_start(src, dst, s_sem, r_sem, first=1, last=31):
        def one(step, carry):
            exchange(src, dst, s_sem, r_sem, step, False).start()
            return carry

        lax.fori_loop(first, last + 1, one, 0)
        if first == 1:
            here = pl.ds(pl.multiple_of(seq * SLOT, SLOT), SLOT)
            dst[here] = src[here]

    def exchange_end(src, dst, s_sem, r_sem):
        def one(step, carry):
            exchange(src, dst, s_sem, r_sem, step, True).wait_recv()
            return carry

        lax.fori_loop(1, 32, one, 0)

    def exchange_sent(src, dst, s_sem, r_sem):
        def one(step, carry):
            exchange(src, dst, s_sem, r_sem, step, False).wait_send()
            return carry

        lax.fori_loop(1, 32, one, 0)

    out_going = (send, got, a_s, a_r)
    far_going = (far_send, far_got, f_s, f_r)
    home_going = (send_b, got_b, e_s, e_r)

    def weight(half, phase, kind, landed):
        along_x = half != phase
        sign = 1 - 2 * half
        wide = phase == 1
        if kind == 0:
            to, piece = sign, (-sign if landed else 0)
        elif kind == 1:
            to, piece = -sign, (sign if landed else 0)
        else:
            to, piece = sign, (2 if landed else -sign)
        part = plane.view(ws, half, wide, along_x, piece)
        return remote(
            part, part, w_s.at[half, phase, kind], w_r.at[half, phase, kind], plane.device(along_x, to)
        )

    def handed(half, phase, index, landed):
        along_x = half != phase
        sign = 1 - 2 * half
        wide = phase == 1
        piece = (0, -sign, sign, 2)[index]
        if landed:
            plane.core = 1 - core
        part = plane.view(ws, half, wide, along_x, piece)
        plane.core = core
        return remote(part, part, b_s.at[half, phase, index], b_r.at[half, phase, index], sibling)

    def weight_near(phase):
        for half in range(2):
            weight(half, phase, 0, True).wait_recv()
            weight(half, phase, 2, False).start()
            handed(half, phase, 1, False).start()
            weight(half, phase, 1, True).wait_recv()
            handed(half, phase, 2, False).start()

    def weight_far(phase):
        for half in range(2):
            weight(half, phase, 2, True).wait_recv()
            if phase == 0:
                weight(half, 1, 0, False).start()
                weight(half, 1, 1, False).start()
            handed(half, phase, 3, False).start()

    for half in range(2):
        weight(half, 0, 0, False).start()
        weight(half, 0, 1, False).start()
        handed(half, 0, 0, False).start()

    send[:, :width] = dot(pick[...], tok[...]).astype(BF16)
    send[:, width : 2 * width] = dot(pick[...], grad[...]).astype(BF16)
    slot_gate = jnp.where(picked, dot(spread, gate_of.astype(BF16)), 0.0)
    slot_gate = jnp.sum(slot_gate, axis=1, keepdims=True)
    send[:, 2 * width :] = jnp.broadcast_to(slot_gate, (slots, 128)).astype(BF16)

    exchange_start(*out_going)

    packed = lax.broadcasted_iota(jnp.int32, pack.shape, 0)
    source = lax.broadcasted_iota(jnp.int32, pack.shape, 1)
    rank = lax.bitwise_and(source, SLOT - 1)
    same = packed == lax.shift_right_logical(source, 4) * MOST + rank
    pack[...] = jnp.where(same & (rank < MOST), 1.0, 0.0).astype(BF16)
    acc_a[...] = jnp.zeros_like(acc_a)
    acc_b[...] = jnp.zeros_like(acc_b)
    acc_u[...] = jnp.zeros_like(acc_u)
    s_acc[...] = jnp.zeros_like(s_acc)
    dg[...] = jnp.zeros_like(dg)

    tokens.land(1)
    weight_near(0)
    tokens.land(2)
    exchange_end(*out_going)
    xb[exp] = dot(pack[...], got[:, :width]).astype(BF16)
    yb[exp] = dot(pack[...], got[:, width : 2 * width]).astype(BF16)
    rows = ZRing((xb.at[exp], yb.at[exp]), (xb, yb), seq, exp, z_s, z_r, 4 - FAR, FAR == 2)
    rows.start(1)
    weight_far(0)
    tokens.land(3)
    tokens.land(4)

    far = [(tx, xb, 4), (ty, yb, 4), (tx, xb, 3), (ty, yb, -3)][: 2 * FAR]
    for copy in own[:2]:
        copy.wait()
    for index, (tokens_of, _, step) in enumerate(far):
        at = slice(index * width, (index + 1) * width)
        far_send[:, at] = dot(pick[...], tokens_of[ring(exp + step, 8)]).astype(BF16)
    exchange_start(*far_going, 1, 8)
    gate[...] = dot(pack[...], got[:, 2 * width :])
    for copy in own[2:]:
        copy.wait()

    def forward(piece):
        cols = pl.ds(pl.multiple_of(piece * width, 128), width)

        acc_a[...] += dot_last(xb[piece], wg[:, cols])
        acc_b[...] += dot_last(xb[piece], wu[:, cols])
        acc_u[...] += dot_last(yb[piece], wd[:, cols])

    def weight_slice(piece, start, size):
        at_x, at_y = lax.div(piece, 2), 2 * lax.rem(piece, 2)
        return ws[at_x, pl.ds(at_y, 2), :, :, start : start + size].reshape(width, size)

    def shared_partial(piece, carry):
        sb[piece] = dot_last(s_dab[...], weight_slice(piece, 0, of_x)).astype(BF16)
        return carry


    def landing(half, phase, kind):
        return qb.at[half, kind] if phase else qa.at[half, kind]

    def reduce_copy(half, phase, kind):
        along_x = half == phase
        sign = 1 - 2 * half
        piece, to = ((2, sign), (-sign, -sign), (sign, sign))[kind]
        return remote(
            plane.view(gp, half, phase == 0, along_x, piece),
            landing(half, phase, kind),
            q_s.at[half, phase, kind],
            q_r.at[half, phase, kind],
            plane.device(along_x, to),
        )

    def reduce_add(half, phase, step, kinds):
        mine = plane.view(gp, half, phase == 0, half == phase, step)
        value = mine[...].astype(F32)
        for kind in kinds:
            value += landing(half, phase, kind)[...].astype(F32)
        mine[...] = value.astype(BF16)

    def reduce_start(phase):
        for half in range(2):
            reduce_copy(half, phase, 0).start()
            reduce_copy(half, phase, 1).start()

    def reduce_pass(phase):
        for half in range(2):
            reduce_copy(half, phase, 0).wait_recv()
            reduce_add(half, phase, 1 - 2 * half, (0,))
            reduce_copy(half, phase, 2).start()

    def reduce_end(phase):
        for half in range(2):
            reduce_copy(half, phase, 1).wait_recv()
            reduce_copy(half, phase, 2).wait_recv()
            reduce_add(half, phase, 0, (1, 2))

    forward(exp)
    weight_near(1)
    exchange_start(*far_going, 9, 16)
    rows.land(1)
    exchange_start(*far_going, 17, 24)
    forward(ring(exp - 1, 8))
    forward(ring(exp + 1, 8))
    weight_far(1)
    exchange_start(*far_going, 25, 31)
    for half in range(2):
        for phase in range(2):
            for index in range(phase, 4):
                handed(half, phase, index, True).wait_recv()

    def shared_forward(piece, carry):
        s_acc[:, :of_x] += dot(tx[piece], weight_slice(piece, 0, of_x))
        s_acc[:, of_x:] += dot(ty[piece], weight_slice(piece, of_x, lanes - of_x))
        return carry

    lax.fori_loop(0, 8, shared_forward, 0)
    act, slope = silu_parts(s_acc[:, :128])
    up, back = s_acc[:, 128:256], s_acc[:, 384:512]
    s_dab[:, :128] = (back * up * slope).astype(BF16)
    s_dab[:, 128:256] = (back * act).astype(BF16)
    s_h[:, :128] = (act * up).astype(BF16)
    act, slope = silu_parts(s_acc[:, 256:384])
    up, back = pltpu.roll(s_acc[:, 256:384], 64, 1), s_acc[:, 512:]
    s_dab[:, 256:] = (back * up * slope + pltpu.roll(back * act, 64, 1)).astype(BF16)
    s_h[:, 128:] = jnp.where(lane < 64, act * up, 0.0).astype(BF16)

    def shared_grads(piece, carry):
        at_x, at_y = lax.div(piece, 2), 2 * lax.rem(piece, 2)
        part = dot_rows(tx[piece], s_dab[...]).astype(BF16)
        gp[at_x, pl.ds(at_y, 2), :, :, :of_x] = part.reshape(2, 2, width // 4, of_x)
        part = dot_rows(ty[piece], s_h[...]).astype(BF16)
        gp[at_x, pl.ds(at_y, 2), :, :, of_x:] = part.reshape(2, 2, width // 4, lanes - of_x)
        return carry

    lax.fori_loop(0, 8, shared_grads, 0)
    across = remote(gp.at[:, :, 1 - core], sib, c_s, c_r, sibling)
    across.start()

    rows.land(2)
    forward(ring(exp - 2, 8))
    forward(ring(exp + 2, 8))
    across.wait_recv()

    def add_sibling(index, carry):
        at_x, at_y = lax.div(index, SIDE), lax.rem(index, SIDE)
        gp[at_x, at_y, core] = (
            gp[at_x, at_y, core].astype(F32) + sib[at_x, at_y].astype(F32)
        ).astype(BF16)
        return carry

    lax.fori_loop(0, SIDE * SIDE, add_sibling, 0)
    reduce_start(0)
    lax.fori_loop(0, 8, shared_partial, 0)
    shared_sums = ZSum(sb, (sp, sm), tok_rows // 2, seq, exp, g_s, g_r)
    shared_sums.step(1)
    exchange_end(*far_going)
    for index, (_, rows_of, step) in enumerate(far):
        at = slice(index * width, (index + 1) * width)
        rows_of[ring(exp + step, 8)] = dot(pack[...], far_got[:, at]).astype(BF16)
    forward(ring(exp + 4, 8))
    rows.land(3)
    shared_sums.step(2)
    forward(ring(exp - 3, 8))
    forward(ring(exp + 3, 8))

    for index in range(count // BLOCK):
        at = pl.ds(index * BLOCK, BLOCK)
        act, slope = silu_parts(acc_a[at])
        up, back = acc_b[at], acc_u[at]
        hidden = act * up
        dg[:, at] = lax.dot_general(
            jnp.ones((16, hidden.shape[1]), F32),
            hidden * back,
            (((1,), (1,)), ((), ())),
            preferred_element_type=F32,
            precision=lax.Precision.HIGHEST,
        ).astype(BF16)
        row_gate = gate[at, 0:1]
        scaled = row_gate * back
        grad_a = (scaled * up * slope).astype(BF16)
        grad_b = (scaled * act).astype(BF16)
        hidden_w = (row_gate * hidden).astype(BF16)
        da[at], db[at], hw[at] = grad_a, grad_b, hidden_w
        dat[:, at], dbt[:, at], hwt[:, at] = grad_a.T, grad_b.T, hidden_w.T

    def partial(piece):
        cols = pl.ds(pl.multiple_of(piece * width, 128), width)
        pb[piece, :count] = (dot(da[...], wg[:, cols]) + dot(db[...], wu[:, cols])).astype(BF16)
        pb[piece, count:] = dg[...]

    row_sums = ZSum(pb, (rp, rm), -(-pb.shape[1] // 32) * 16, seq, exp, p_s, p_r)

    outs = (out_gate, out_up, out_down)

    def out_copy(index, which):
        piece = ring(exp + index, 8)
        cols = pl.ds(pl.multiple_of(piece * width, 128), width)
        return pltpu.make_async_copy(
            stage.at[index % 2, which], outs[which].at[:, cols], o_s.at[index % 2, which]
        )

    def weight_grads(index):
        piece = ring(exp + index, 8)
        if index >= 2:
            for which in range(3):
                out_copy(index - 2, which).wait()
        stage[index % 2, 0] = dot(dat[...], xb[piece]).astype(BF16)
        stage[index % 2, 1] = dot(dbt[...], xb[piece]).astype(BF16)
        stage[index % 2, 2] = dot(hwt[...], yb[piece]).astype(BF16)
        for which in range(3):
            out_copy(index, which).start()

    partial(ring(exp + 4, 8))
    row_sums.step(1)
    partial(ring(exp + 3, 8))
    partial(ring(exp - 3, 8))
    row_sums.step(2)
    reduce_pass(0)
    partial(ring(exp + 2, 8))
    partial(ring(exp - 2, 8))
    weight_grads(0)
    row_sums.step(3)
    reduce_end(0)
    reduce_start(1)
    partial(ring(exp + 1, 8))
    partial(ring(exp - 1, 8))
    weight_grads(1)
    weight_grads(2)
    weight_grads(3)
    row_sums.step(4)
    shared_sums.step(3)
    reduce_pass(1)
    partial(exp)
    for index in range(4, 8):
        weight_grads(index)
    whole = row_sums.total()

    send_b[:, :width] = dot_rows(pack[...], whole[:count].astype(BF16)).astype(BF16)
    route = whole[count : count + 16, :count].T[:, 0:1]
    route = jnp.broadcast_to(route, (count, 128)).astype(BF16)
    send_b[:, width:] = dot_rows(pack[...], route).astype(BF16)
    exchange_start(*home_going)
    shared_sums.step(4)

    tokens.finish()
    rows.finish()
    row_sums.finish()
    reduce_end(1)
    out_shared[...] = gp[plane.x, plane.y, core]
    exchange_sent(*out_going)
    exchange_sent(*far_going)
    across.wait_send()
    for half in range(2):
        for phase in range(2):
            for kind in range(3):
                weight(half, phase, kind, False).wait_send()
                reduce_copy(half, phase, kind).wait_send()
            for index in range(phase, 4):
                handed(half, phase, index, False).wait_send()
    for index in (6, 7):
        for which in range(3):
            out_copy(index, which).wait()

    shared_rows = shared_sums.total()
    exchange_end(*home_going)
    out_tok[...] = (dot_rows(pick[...], got_b[:, :width]) + shared_rows).astype(BF16)
    routes = jnp.where(picked, got_b[:, width:].astype(F32), 0.0).astype(BF16)
    routes = dot_rows(spread, routes)
    for k in range(ids.shape[0]):
        hit = jnp.where(ids[k : k + 1] == expert, routes, 0.0)
        out_route[k : k + 1] = jnp.sum(hit, axis=0, keepdims=True)
    exchange_sent(*home_going)
    shared_sums.finish()


def any_specs(count):
    return [pl.BlockSpec(memory_space=pl.ANY)] * count


def vmem_specs(count):
    return [pl.BlockSpec(memory_space=pltpu.VMEM)] * count


def layer(ids, gates, tok, grad, w_gate, w_up, w_down, shared_gate, shared_up, shared_down):
    hidden, model = w_gate.shape
    tok_rows, width = tok.shape
    experts = model // shared_gate.shape[0]
    slots, count = experts * SLOT, experts * MOST
    chunk, lanes, of_x = shared_gate.shape[0], 640, 384
    dma = pltpu.SemaphoreType.DMA
    vmem = pltpu.VMEM
    routed = jax.ShapeDtypeStruct((hidden, model), BF16)
    return pl.pallas_call(
        layer_kernel,
        out_shape=(
            jax.ShapeDtypeStruct((tok_rows, width), BF16),
            jax.ShapeDtypeStruct(ids.shape, F32),
            routed,
            routed,
            routed,
            jax.ShapeDtypeStruct((chunk, lanes), BF16),
        ),
        in_specs=vmem_specs(4) + any_specs(3) + vmem_specs(3),
        out_specs=vmem_specs(2) + any_specs(3) + vmem_specs(1),
        scratch_shapes=[
            vmem((slots, tok_rows), BF16),
            vmem((slots, 2 * width + 128), BF16),
            vmem((slots, 2 * width + 128), BF16),
            vmem((slots, 2 * FAR * width), BF16),
            vmem((slots, 2 * FAR * width), BF16),
            vmem((count, slots), BF16),
            vmem((count, 128), F32),
            vmem((8, count, width), BF16),
            vmem((8, count, width), BF16),
            vmem((hidden, model), BF16),
            vmem((hidden, model), BF16),
            vmem((hidden, model), BF16),
            vmem((8, tok_rows, width), BF16),
            vmem((8, tok_rows, width), BF16),
            vmem((SIDE, SIDE, 2, chunk, lanes), BF16),
            vmem((tok_rows, lanes), F32),
            vmem((tok_rows, of_x), BF16),
            vmem((tok_rows, lanes - of_x), BF16),
            vmem((SIDE, SIDE, 2, chunk, lanes), BF16),
            vmem((SIDE, SIDE, chunk, lanes), BF16),
            vmem((2, 3, SIDE, chunk // 2, lanes), BF16),
            vmem((2, 3, chunk // 2, lanes), BF16),
            vmem((count, hidden), F32),
            vmem((count, hidden), F32),
            vmem((count, hidden), F32),
            vmem((count, hidden), BF16),
            vmem((count, hidden), BF16),
            vmem((count, hidden), BF16),
            vmem((hidden, count), BF16),
            vmem((hidden, count), BF16),
            vmem((hidden, count), BF16),
            vmem((16, width), BF16),
            vmem((8, count + 16, width), BF16),
            vmem((4, count + 16, width), BF16),
            vmem((4, count + 16, width), BF16),
            vmem((8, tok_rows, width), BF16),
            vmem((4, tok_rows, width), BF16),
            vmem((4, tok_rows, width), BF16),
            vmem((2, 3, hidden, width), BF16),
            vmem((slots, width + 128), BF16),
            vmem((slots, width + 128), BF16),
            dma((5,)),
            dma((31,)),
            dma((31,)),
            dma((31,)),
            dma((31,)),
            dma((2, 2, 4)),
            dma((2, 2, 4)),
            dma((2, 2, 3)),
            dma((2, 2, 3)),
            dma((2, 2, 4)),
            dma((2, 2, 4)),
            dma((2, 2, 4)),
            dma((2, 2, 4)),
            dma,
            dma,
            dma((2, 2, 3)),
            dma((2, 2, 3)),
            dma((2, 2, 4)),
            dma((2, 2, 4)),
            dma((2, 2, 4)),
            dma((2, 2, 4)),
            dma((2, 3)),
            dma((31,)),
            dma((31,)),
        ],
        compiler_params=pltpu.CompilerParams(
            collective_id=0, has_side_effects=True, vmem_limit_bytes=62 * MIB
        ),
    )(ids, gates, tok, grad, w_gate, w_up, w_down, shared_gate, shared_up, shared_down)


PARTS = 4


def finish_kernel(
    tok, route, shared, in_gate, in_up, in_down,
    out_tok, out_route, out_gate, out_up, out_down, shared_gate, shared_up, shared_down,
):
    out_gate[...] = in_gate[...]
    out_up[...] = in_up[...]
    out_down[...] = in_down[...]

    @pl.when(pl.program_id(0) == 0)
    def _():
        out_tok[...] = tok[...]
        out_route[...] = route[...]
        units = shared_gate.shape[1]
        shared_gate[:, :128] = shared[:, :128]
        shared_gate[:, 128:] = shared[:, 256 : 256 + units - 128]
        shared_up[:, :128] = shared[:, 128:256]
        shared_up[:, 128:] = dot(shared[:, 256:384], one_hot(128, units - 128, 64)).astype(BF16)
        shared_down[:, :128] = shared[:, 384:512]
        shared_down[:, 128:] = shared[:, 512 : 512 + units - 128]


def finish(tok, route, shared, grads, shared_shapes):
    shapes = [tok, route, *grads, *shared_shapes]
    hidden, model = grads[0].shape

    def whole(part):
        return pl.BlockSpec(part.shape, lambda step: (0, 0))

    band = [pl.BlockSpec((hidden // PARTS, model), lambda step: (step, 0))] * 3
    return pl.pallas_call(
        finish_kernel,
        grid=(PARTS,),
        out_shape=tuple(jax.ShapeDtypeStruct(part.shape, part.dtype) for part in shapes),
        in_specs=[whole(tok), whole(route), whole(shared), *band],
        out_specs=[whole(tok), whole(route), *band, *map(whole, shared_shapes)],
        compiler_params=pltpu.CompilerParams(vmem_limit_bytes=62 * MIB),
    )(tok, route, shared, *grads)


def body(
    tokens, out_grad, expert_ids, gates, w_gate, w_up, w_down, shared_gate, shared_up, shared_down
):
    shared = (shared_gate, shared_up, shared_down.T)
    token_grad, route, grad_gate, grad_up, grad_down, grad_shared = layer(
        expert_ids.T, gates.T, tokens, out_grad, w_gate[0], w_up[0], w_down[0], *shared
    )
    token_grad, route, grad_gate, grad_up, grad_down, *grads = finish(
        token_grad, route, grad_shared, (grad_gate, grad_up, grad_down), shared
    )
    return (
        token_grad,
        route.T,
        grad_gate[None],
        grad_up[None],
        grad_down[None],
        grads[0],
        grads[1],
        grads[2].T,
    )


def solution(mesh):
    return jax.shard_map(
        body,
        mesh=mesh,
        in_specs=(
            P("seq", "exp"),
            P("seq", "exp"),
            P("seq", None),
            P("seq", None),
            P("seq", "exp", None),
            P("seq", "exp", None),
            P("seq", "exp", None),
            P("seq", "exp"),
            P("seq", "exp"),
            P("exp", "seq"),
        ),
        out_specs=(
            P("seq", "exp"),
            P("seq", None),
            P("seq", "exp", None),
            P("seq", "exp", None),
            P("seq", "exp", None),
            P("seq", "exp"),
            P("seq", "exp"),
            P("exp", "seq"),
        ),
        check_vma=False,
    )
```

```python
import functools

import jax
import jax.numpy as jnp
from jax import lax
from jax.experimental import pallas as pl
from jax.experimental.pallas import tpu as pltpu
from jax.sharding import PartitionSpec as P

MESH = pl.DeviceIdType.MESH
MOST = 12
SLOT = 16
SIDE = 4
BLOCK = 128
FAR = 2
MIB = 1 << 20
F32 = jnp.float32
BF16 = jnp.bfloat16


def dot(left, right):
    return jnp.dot(left, right, preferred_element_type=F32)


def dot_last(left, right):
    return lax.dot_general(left, right, (((1,), (1,)), ((), ())), preferred_element_type=F32)


def dot_rows(left, right):
    return lax.dot_general(left, right, (((0,), (0,)), ((), ())), preferred_element_type=F32)


def silu_parts(value):
    sig = jax.nn.sigmoid(value)
    return value * sig, sig * (1.0 + value * (1.0 - sig))


def ring(value, size):
    return lax.rem(value + size, size)


def place():
    seq, exp = lax.axis_index("seq"), lax.axis_index("exp")
    return (
        seq,
        exp,
        lax.div(seq, 2 * SIDE),
        lax.rem(lax.div(seq, 2), SIDE),
        lax.rem(seq, 2),
    )


def remote(src, dst, send_sem, recv_sem, device):
    return pltpu.make_async_remote_copy(
        src_ref=src,
        dst_ref=dst,
        send_sem=send_sem,
        recv_sem=recv_sem,
        device_id=device,
        device_id_type=MESH,
    )


def greet(barrier, device):
    pl.semaphore_signal(barrier, inc=1, device_id=device, device_id_type=MESH)


class ZRing:
    def __init__(self, own, bufs, seq, exp, send_sem, recv_sem, full=3, half=True):
        self.own, self.bufs, self.seq, self.exp = own, bufs, seq, exp
        self.send_sem, self.recv_sem = send_sem, recv_sem
        self.full, self.half = full, half

    def has(self, step, way, sub):
        return step <= self.full or (self.half and step == self.full + 1 and way == sub)

    def copy(self, step, way, sub, landed=False):
        sign = 1 - 2 * way
        piece = ring(self.exp - sign * (step if landed else step - 1), 8)
        slot = self.bufs[sub].at[piece]
        src = self.own[sub] if step == 1 and not landed else slot
        return remote(
            src,
            slot,
            self.send_sem.at[way, sub, step - 1],
            self.recv_sem.at[way, sub, step - 1],
            (self.seq, ring(self.exp + sign, 8)),
        )

    def start(self, step, *subs):
        for sub in subs or range(2):
            for way in range(2):
                if self.has(step, way, sub):
                    self.copy(step, way, sub).start()

    def land(self, step):
        for sub in range(2):
            for way in range(2):
                if self.has(step, way, sub):
                    self.copy(step, way, sub, landed=True).wait_recv()
                    if self.has(step + 1, way, sub):
                        self.copy(step + 1, way, sub).start()

    def finish(self):
        for step in range(1, 5):
            for sub in range(2):
                for way in range(2):
                    if self.has(step, way, sub):
                        self.copy(step, way, sub).wait_send()


class ZSum:
    def __init__(self, own, landed, split, seq, exp, send_sem, recv_sem):
        self.own, self.landed, self.seq, self.exp = own, landed, seq, exp
        self.send_sem, self.recv_sem = send_sem, recv_sem
        self.parts = (pl.ds(0, split), pl.ds(split, own.shape[1] - split))

    def has(self, step, way, sub):
        return step > 1 or way == sub

    def copy(self, step, way, sub):
        sign = 1 - 2 * way
        return remote(
            self.own.at[ring(self.exp + sign * (5 - step), 8), self.parts[sub]],
            self.landed[way].at[step - 1, self.parts[sub]],
            self.send_sem.at[way, sub, step - 1],
            self.recv_sem.at[way, sub, step - 1],
            (self.seq, ring(self.exp + sign, 8)),
        )

    def step(self, step):
        for sub in range(2):
            for way in range(2):
                if step > 1 and self.has(step - 1, way, sub):
                    self.copy(step - 1, way, sub).wait_recv()
                    piece = ring(self.exp + (1 - 2 * way) * (5 - step), 8)
                    part = self.parts[sub]
                    self.own[piece, part] = (
                        self.own[piece, part].astype(F32) + self.landed[way][step - 2, part].astype(F32)
                    ).astype(BF16)
                if self.has(step, way, sub):
                    self.copy(step, way, sub).start()

    def total(self):
        for sub in range(2):
            for way in range(2):
                self.copy(4, way, sub).wait_recv()
        return sum(part.astype(F32) for part in (self.own[self.exp], self.landed[0][3], self.landed[1][3]))

    def finish(self):
        for step in range(1, 5):
            for way in range(2):
                for sub in range(2):
                    if self.has(step, way, sub):
                        self.copy(step, way, sub).wait_send()


BANDS = ((0, 48, False, 1), (48, 32, False, -1), (80, 48, True, -1), (128, 32, True, 1))


class Plane:
    def __init__(self):
        self.seq, self.exp, self.x, self.y, self.core = place()

    def device(self, along_x, step):
        x = ring(self.x + step, SIDE) if along_x else self.x
        y = self.y if along_x else ring(self.y + step, SIDE)
        return ((x * SIDE + y) * 2 + self.core, self.exp)

    def view(self, ref, band, wide, along_x, step):
        rows = pl.ds(BANDS[band][0], BANDS[band][1])
        here = ring((self.x if along_x else self.y) + step, SIDE)
        if along_x:
            return ref.at[here, :, self.core, rows] if wide else ref.at[here, self.y, self.core, rows]
        return ref.at[:, here, self.core, rows] if wide else ref.at[self.x, here, self.core, rows]


def one_hot(rows, columns, shift):
    row = lax.broadcasted_iota(jnp.int32, (rows, columns), 0)
    column = lax.broadcasted_iota(jnp.int32, (rows, columns), 1)
    return jnp.where(row == column + shift, 1.0, 0.0).astype(BF16)


def half_lanes(rows, high):
    lane = lax.broadcasted_iota(jnp.int32, (rows, 128), 1)
    return jnp.where((lane >= 64) == high, 1.0, 0.0).astype(BF16)


def layer_kernel(
    ids, gates, tok, grad, w_gate, w_up, w_down, shared_gate, shared_up, shared_down,
    out_tok, out_route, out_gate, out_up, out_down, out_shared,
    pick, spare, send, got, far_send, far_got, pack, gate, xb, yb, wg, wu, wd, tx, ty, ws,
    s_acc, s_dab, s_h, gp, sib, qa, qb,
    acc_a, acc_b, acc_u, da, db, hw, dat, dbt, hwt, dg,
    pb, rp, rm, sb, sp, sm, got_b,
    own_sem, a_s, a_r, f_s, f_r, t_s, t_r, w_s, w_r, b_s, b_r, z_s, z_r, c_s, c_r, q_s, q_r,
    p_s, p_r, g_s, g_r, o_s, e_s, e_r,
):
    plane = Plane()
    seq, exp, core = plane.seq, plane.exp, plane.core
    sibling = (seq + 1 - 2 * core, exp)
    count = pack.shape[0]
    tok_rows, width = tok.shape
    slots = send.shape[0]
    of_x, lanes = s_dab.shape[1], ws.shape[4]

    own = [
        pltpu.make_async_copy(src, dst, own_sem.at[i])
        for i, (src, dst) in enumerate(
            ((tok, tx.at[exp]), (grad, ty.at[exp]), (w_gate, wg), (w_up, wu), (w_down, wd))
        )
    ]
    for copy in own:
        copy.start()

    barrier = pltpu.get_barrier_semaphore()

    def hello(step, carry):
        greet(barrier, (ring(seq + step, 32), exp))
        return carry

    lax.fori_loop(1, 32, hello, 0)
    greet(barrier, (seq, ring(exp + 1, 8)))
    greet(barrier, (seq, ring(exp - 1, 8)))

    experts = slots // SLOT
    expert = lax.broadcasted_iota(jnp.int32, (experts, tok_rows), 0)
    named = jnp.zeros((experts, tok_rows), F32)
    gate_of = jnp.zeros((experts, tok_rows), F32)
    for k in range(ids.shape[0]):
        hit = ids[k : k + 1] == expert
        named += jnp.where(hit, 1.0, 0.0)
        gate_of += jnp.where(hit, gates[k : k + 1].astype(F32), 0.0)
    row = lax.broadcasted_iota(jnp.int32, (tok_rows, tok_rows), 0)
    lane = lax.broadcasted_iota(jnp.int32, (tok_rows, tok_rows), 1)
    earlier = jnp.where(row < lane, 1.0, 0.0)
    rank = jnp.where(named > 0.0, dot(named.astype(BF16), earlier.astype(BF16)), -1.0)
    slot = lax.broadcasted_iota(jnp.int32, (slots, experts), 0)
    to_expert = lax.shift_right_logical(slot, 4) == lax.broadcasted_iota(jnp.int32, (slots, experts), 1)
    spread = jnp.where(to_expert, 1.0, 0.0).astype(BF16)
    slot = lax.broadcasted_iota(jnp.int32, (slots, tok_rows), 0)
    slot_rank = lax.bitwise_and(slot, SLOT - 1)
    rank_of = dot(spread, rank.astype(BF16))
    picked = rank_of == slot_rank.astype(F32)
    pick[...] = jnp.where(picked, 1.0, 0.0).astype(BF16)
    for third in range(3):
        moved = rank_of == (slot_rank - MOST + 4 * third).astype(F32)
        spare[third] = jnp.where(moved & (slot_rank >= MOST), 1.0, 0.0).astype(BF16)

    units = shared_gate.shape[1]
    ws[plane.x, plane.y, core, :, :128] = shared_gate[:, :128]
    ws[plane.x, plane.y, core, :, 128:256] = shared_up[:, :128]
    ws[plane.x, plane.y, core, :, 256:384] = (
        dot(shared_gate[...], one_hot(units, 128, 128)) + dot(shared_up[...], one_hot(units, 128, 64) * half_lanes(units, True))
    ).astype(BF16)
    ws[plane.x, plane.y, core, :, 384:512] = shared_down[:, :128]
    ws[plane.x, plane.y, core, :, 512:] = dot(shared_down[...], one_hot(units, 128, 128)).astype(BF16)
    pl.semaphore_wait(barrier, 33)

    tokens = ZRing((tok, grad), (tx, ty), seq, exp, t_s, t_r)
    tokens.start(1)

    def exchange(src, dst, s_sem, r_sem, step, landed):
        to, source = ring(seq + step, 32), ring(seq - step, 32)
        at = (source if landed else seq) * SLOT
        return remote(
            src.at[pl.ds(pl.multiple_of(to * SLOT, SLOT), SLOT)],
            dst.at[pl.ds(pl.multiple_of(at, SLOT), SLOT)],
            s_sem.at[step - 1],
            r_sem.at[step - 1],
            (to, exp),
        )

    def exchange_start(src, dst, s_sem, r_sem, first=1, last=31):
        def one(step, carry):
            exchange(src, dst, s_sem, r_sem, step, False).start()
            return carry

        lax.fori_loop(first, last + 1, one, 0)
        if first == 1:
            here = pl.ds(pl.multiple_of(seq * SLOT, SLOT), SLOT)
            dst[here] = src[here]

    def exchange_end(src, dst, s_sem, r_sem):
        def one(step, carry):
            exchange(src, dst, s_sem, r_sem, step, True).wait_recv()
            return carry

        lax.fori_loop(1, 32, one, 0)

    def exchange_sent(src, dst, s_sem, r_sem):
        def one(step, carry):
            exchange(src, dst, s_sem, r_sem, step, False).wait_send()
            return carry

        lax.fori_loop(1, 32, one, 0)

    out_going = (send, got, a_s, a_r)
    far_going = (far_send, far_got, f_s, f_r)
    send_b = send.at[:, : width + 128]
    home_going = (send_b, got_b, e_s, e_r)

    def weight(band, phase, kind, landed):
        along_x = BANDS[band][2] != (phase == 1)
        sign = BANDS[band][3]
        wide = phase == 1
        if kind == 0:
            to, piece = sign, (-sign if landed else 0)
        elif kind == 1:
            to, piece = -sign, (sign if landed else 0)
        else:
            to, piece = sign, (2 if landed else -sign)
        part = plane.view(ws, band, wide, along_x, piece)
        return remote(
            part, part, w_s.at[band, phase, kind], w_r.at[band, phase, kind], plane.device(along_x, to)
        )

    def handed(band, phase, index, landed):
        along_x = BANDS[band][2] != (phase == 1)
        sign = BANDS[band][3]
        wide = phase == 1
        piece = (0, -sign, sign, 2)[index]
        if landed:
            plane.core = 1 - core
        part = plane.view(ws, band, wide, along_x, piece)
        plane.core = core
        return remote(part, part, b_s.at[band, phase, index], b_r.at[band, phase, index], sibling)

    def weight_near(phase):
        for band in range(4):
            weight(band, phase, 0, True).wait_recv()
            weight(band, phase, 2, False).start()
            handed(band, phase, 1, False).start()
            weight(band, phase, 1, True).wait_recv()
            handed(band, phase, 2, False).start()

    def weight_far(phase):
        for band in range(4):
            weight(band, phase, 2, True).wait_recv()
            if phase == 0:
                weight(band, 1, 0, False).start()
                weight(band, 1, 1, False).start()
            handed(band, phase, 3, False).start()

    send[:, :width] = dot(pick[...], tok[...]).astype(BF16)
    send[:, width : 2 * width] = dot(pick[...], grad[...]).astype(BF16)
    slot_gate = jnp.where(picked, dot(spread, gate_of.astype(BF16)), 0.0)
    slot_gate = jnp.sum(slot_gate, axis=1, keepdims=True)
    send[:, 2 * width :] = jnp.broadcast_to(slot_gate, (slots, 128)).astype(BF16)

    exchange_start(*out_going)
    for band in range(4):
        weight(band, 0, 0, False).start()
        weight(band, 0, 1, False).start()
        handed(band, 0, 0, False).start()

    packed = lax.broadcasted_iota(jnp.int32, pack.shape, 0)
    source = lax.broadcasted_iota(jnp.int32, pack.shape, 1)
    rank = lax.bitwise_and(source, SLOT - 1)
    same = packed == lax.shift_right_logical(source, 4) * MOST + rank
    pack[...] = jnp.where(same & (rank < MOST), 1.0, 0.0).astype(BF16)
    acc_a[...] = jnp.zeros_like(acc_a)
    acc_b[...] = jnp.zeros_like(acc_b)
    acc_u[...] = jnp.zeros_like(acc_u)
    s_acc[...] = jnp.zeros_like(s_acc)
    dg[...] = jnp.zeros_like(dg)

    tokens.land(1)
    tokens.land(2)
    exchange_end(*out_going)
    rows = ZRing((xb.at[exp], yb.at[exp]), (xb, yb), seq, exp, z_s, z_r, 4 - FAR, FAR == 2)
    xb[exp] = dot(pack[...], got[:, :width]).astype(BF16)
    rows.start(1, 0)
    yb[exp] = dot(pack[...], got[:, width : 2 * width]).astype(BF16)
    rows.start(1, 1)
    weight_near(0)
    weight_far(0)
    tokens.land(3)
    tokens.land(4)

    far = [(tx, xb, 4), (ty, yb, 4), (tx, xb, 3), (ty, yb, -3)][: 2 * FAR]
    for copy in own[:2]:
        copy.wait()
    tiles = width // 128
    spare_of, _, spare_step = far[3]
    spare_of = spare_of[ring(exp + spare_step, 8)]
    thirds = [dot(spare[third], spare_of) for third in range(3)]
    for index, (tokens_of, _, step) in enumerate(far[:3]):
        plain = dot(pick[...], tokens_of[ring(exp + step, 8)])
        for tile in range(tiles):
            column = index * tiles + tile
            extra = thirds[column % 3][:, column // 3 * 128 : column // 3 * 128 + 128]
            far_send[:, column * 128 : column * 128 + 128] = (
                plain[:, tile * 128 : tile * 128 + 128] + extra
            ).astype(BF16)
    exchange_start(*far_going, 1, 8)
    gate[...] = dot(pack[...], got[:, 2 * width :]).astype(BF16)
    for copy in own[2:]:
        copy.wait()

    def forward(piece):
        cols = pl.ds(pl.multiple_of(piece * width, 128), width)

        acc_a[...] += dot_last(xb[piece], wg[:, cols])
        acc_b[...] += dot_last(xb[piece], wu[:, cols])
        acc_u[...] += dot_last(yb[piece], wd[:, cols])

    def weight_slice(piece, start, size):
        at_x, at_y = lax.div(piece, 2), 2 * lax.rem(piece, 2)
        return ws[at_x, pl.ds(at_y, 2), :, :, start : start + size].reshape(width, size)

    def shared_partial(piece, carry):
        sb[piece] = dot_last(s_dab[...], weight_slice(piece, 0, of_x)).astype(BF16)
        return carry


    def landing(band, phase, kind):
        size = pl.ds(0, BANDS[band][1])
        return qb.at[band, kind, size] if phase else qa.at[band, kind, :, size]

    def reduce_copy(band, phase, kind):
        along_x = BANDS[band][2] == (phase == 1)
        sign = BANDS[band][3]
        piece, to = ((2, sign), (-sign, -sign), (sign, sign))[kind]
        return remote(
            plane.view(gp, band, phase == 0, along_x, piece),
            landing(band, phase, kind),
            q_s.at[band, phase, kind],
            q_r.at[band, phase, kind],
            plane.device(along_x, to),
        )

    def reduce_add(band, phase, step, kinds):
        mine = plane.view(gp, band, phase == 0, BANDS[band][2] == (phase == 1), step)
        value = mine[...].astype(F32)
        for kind in kinds:
            value += landing(band, phase, kind)[...].astype(F32)
        mine[...] = value.astype(BF16)

    def reduce_start(phase):
        for band in range(4):
            reduce_copy(band, phase, 0).start()
            reduce_copy(band, phase, 1).start()

    def reduce_pass(phase):
        for band in range(4):
            reduce_copy(band, phase, 0).wait_recv()
            reduce_add(band, phase, BANDS[band][3], (0,))
            reduce_copy(band, phase, 2).start()

    def reduce_end(phase):
        for band in range(4):
            reduce_copy(band, phase, 1).wait_recv()
            reduce_copy(band, phase, 2).wait_recv()
            reduce_add(band, phase, 0, (1, 2))

    forward(exp)
    weight_near(1)
    exchange_start(*far_going, 9, 16)
    rows.land(1)
    exchange_start(*far_going, 17, 24)
    forward(ring(exp - 1, 8))
    forward(ring(exp + 1, 8))
    exchange_start(*far_going, 25, 31)
    rows.land(2)
    forward(ring(exp - 2, 8))
    forward(ring(exp + 2, 8))
    weight_far(1)
    for band in range(4):
        for phase in range(2):
            for index in range(phase, 4):
                handed(band, phase, index, True).wait_recv()

    def shared_forward(piece, carry):
        s_acc[:, :of_x] += dot(tx[piece], weight_slice(piece, 0, of_x))
        s_acc[:, of_x:] += dot(ty[piece], weight_slice(piece, of_x, lanes - of_x))
        return carry

    lax.fori_loop(0, 8, shared_forward, 0)
    act, slope = silu_parts(s_acc[:, :128])
    up, back = s_acc[:, 128:256], s_acc[:, 384:512]
    s_dab[:, :128] = (back * up * slope).astype(BF16)
    s_dab[:, 128:256] = (back * act).astype(BF16)
    s_h[:, :128] = (act * up).astype(BF16)
    act, slope = silu_parts(s_acc[:, 256:384])
    up, back = pltpu.roll(s_acc[:, 256:384], 64, 1), s_acc[:, 512:]
    s_dab[:, 256:] = (back * up * slope + pltpu.roll(back * act, 64, 1)).astype(BF16)
    s_h[:, 128:] = jnp.where(lane < 64, act * up, 0.0).astype(BF16)

    def shared_grads(piece, carry):
        at_x, at_y = lax.div(piece, 2), 2 * lax.rem(piece, 2)
        part = dot_rows(tx[piece], s_dab[...]).astype(BF16)
        gp[at_x, pl.ds(at_y, 2), :, :, :of_x] = part.reshape(2, 2, width // 4, of_x)
        part = dot_rows(ty[piece], s_h[...]).astype(BF16)
        gp[at_x, pl.ds(at_y, 2), :, :, of_x:] = part.reshape(2, 2, width // 4, lanes - of_x)
        return carry

    lax.fori_loop(0, 8, shared_grads, 0)
    across = remote(gp.at[:, :, 1 - core], sib, c_s, c_r, sibling)
    across.start()

    exchange_end(*far_going)
    for index, (_, rows_of, step) in enumerate(far[:3]):
        at = slice(index * width, (index + 1) * width)
        rows_of[ring(exp + step, 8)] = dot(pack[...], far_got[:, at]).astype(BF16)
    value = 0.0
    for third in range(3):
        columns = [third + 3 * tile for tile in range(tiles)]
        part = jnp.concatenate([far_got[:, c * 128 : c * 128 + 128] for c in columns], axis=1)
        packed = lax.broadcasted_iota(jnp.int32, pack.shape, 0)
        source = lax.broadcasted_iota(jnp.int32, pack.shape, 1)
        rank = lax.bitwise_and(source, SLOT - 1)
        moved = packed == lax.shift_right_logical(source, 4) * MOST + rank - MOST + 4 * third
        value += dot(jnp.where(moved & (rank >= MOST), 1.0, 0.0).astype(BF16), part)
    far[3][1][ring(exp + far[3][2], 8)] = value.astype(BF16)
    forward(ring(exp + 4, 8))
    rows.land(3)
    forward(ring(exp - 3, 8))
    forward(ring(exp + 3, 8))

    for index in range(count // BLOCK):
        at = pl.ds(index * BLOCK, BLOCK)
        act, slope = silu_parts(acc_a[at])
        up, back = acc_b[at], acc_u[at]
        hidden = act * up
        dg[:, at] = lax.dot_general(
            jnp.ones((16, hidden.shape[1]), F32),
            hidden * back,
            (((1,), (1,)), ((), ())),
            preferred_element_type=F32,
            precision=lax.Precision.HIGHEST,
        ).astype(BF16)
        row_gate = gate[at, 0:1].astype(F32)
        scaled = row_gate * back
        grad_a = (scaled * up * slope).astype(BF16)
        grad_b = (scaled * act).astype(BF16)
        hidden_w = (row_gate * hidden).astype(BF16)
        da[at], db[at], hw[at] = grad_a, grad_b, hidden_w
        dat[:, at], dbt[:, at], hwt[:, at] = grad_a.T, grad_b.T, hidden_w.T

    def partial(piece):
        cols = pl.ds(pl.multiple_of(piece * width, 128), width)
        pb[piece, :count] = (dot(da[...], wg[:, cols]) + dot(db[...], wu[:, cols])).astype(BF16)
        pb[piece, count:] = dg[...]

    row_sums = ZSum(pb, (rp, rm), -(-pb.shape[1] // 32) * 16, seq, exp, p_s, p_r)

    outs = (out_gate, out_up, out_down)
    hidden = dat.shape[0]

    def stage(index, which):
        return far_got.at[
            index % 2 * hidden : (index % 2 + 1) * hidden, which * width : (which + 1) * width
        ]

    def out_copy(index, which):
        piece = ring(exp + index, 8)
        cols = pl.ds(pl.multiple_of(piece * width, 128), width)
        return pltpu.make_async_copy(
            stage(index, which), outs[which].at[:, cols], o_s.at[index % 2, which]
        )

    def weight_grads(index):
        piece = ring(exp + index, 8)
        if index >= 2:
            for which in range(3):
                out_copy(index - 2, which).wait()
        stage(index, 0)[...] = dot(dat[...], xb[piece]).astype(BF16)
        stage(index, 1)[...] = dot(dbt[...], xb[piece]).astype(BF16)
        stage(index, 2)[...] = dot(hwt[...], yb[piece]).astype(BF16)
        for which in range(3):
            out_copy(index, which).start()

    partial(ring(exp + 4, 8))
    row_sums.step(1)
    lax.fori_loop(0, 8, shared_partial, 0)
    shared_sums = ZSum(sb, (sp, sm), tok_rows // 2, seq, exp, g_s, g_r)
    shared_sums.step(1)
    partial(ring(exp + 3, 8))
    partial(ring(exp - 3, 8))
    row_sums.step(2)

    def add_sibling(index, carry):
        at_x, at_y = lax.div(index, SIDE), lax.rem(index, SIDE)
        gp[at_x, at_y, core] = (
            gp[at_x, at_y, core].astype(F32) + sib[at_x, at_y].astype(F32)
        ).astype(BF16)
        return carry

    across.wait_recv()
    lax.fori_loop(0, SIDE * SIDE, add_sibling, 0)
    reduce_start(0)
    partial(ring(exp + 2, 8))
    partial(ring(exp - 2, 8))
    weight_grads(0)
    row_sums.step(3)
    shared_sums.step(2)
    partial(ring(exp + 1, 8))
    partial(ring(exp - 1, 8))
    weight_grads(1)
    weight_grads(2)
    reduce_pass(0)
    row_sums.step(4)
    shared_sums.step(3)
    partial(exp)
    for index in range(3, 8):
        weight_grads(index)
    reduce_end(0)
    reduce_start(1)
    whole = row_sums.total()

    exchange_sent(*out_going)
    send_b[:, :width] = dot_rows(pack[...], whole[:count].astype(BF16)).astype(BF16)
    route = whole[count : count + 16, :count].T[:, 0:1]
    route = jnp.broadcast_to(route, (count, 128)).astype(BF16)
    send_b[:, width:] = dot_rows(pack[...], route).astype(BF16)
    exchange_start(*home_going)
    shared_sums.step(4)
    reduce_pass(1)

    tokens.finish()
    rows.finish()
    row_sums.finish()
    reduce_end(1)
    out_shared[...] = gp[plane.x, plane.y, core]
    exchange_sent(*far_going)
    across.wait_send()
    for band in range(4):
        for phase in range(2):
            for kind in range(3):
                weight(band, phase, kind, False).wait_send()
                reduce_copy(band, phase, kind).wait_send()
            for index in range(phase, 4):
                handed(band, phase, index, False).wait_send()
    for index in (6, 7):
        for which in range(3):
            out_copy(index, which).wait()

    shared_rows = shared_sums.total()
    exchange_end(*home_going)
    out_tok[...] = (dot_rows(pick[...], got_b[:, :width]) + shared_rows).astype(BF16)
    routes = jnp.where(picked, got_b[:, width:].astype(F32), 0.0).astype(BF16)
    routes = dot_rows(spread, routes)
    for k in range(ids.shape[0]):
        hit = jnp.where(ids[k : k + 1] == expert, routes, 0.0)
        out_route[k : k + 1] = jnp.sum(hit, axis=0, keepdims=True)
    exchange_sent(*home_going)
    shared_sums.finish()


def any_specs(count):
    return [pl.BlockSpec(memory_space=pl.ANY)] * count


def vmem_specs(count):
    return [pl.BlockSpec(memory_space=pltpu.VMEM)] * count


def layer(ids, gates, tok, grad, w_gate, w_up, w_down, shared_gate, shared_up, shared_down):
    hidden, model = w_gate.shape
    tok_rows, width = tok.shape
    experts = model // shared_gate.shape[0]
    slots, count = experts * SLOT, experts * MOST
    chunk, lanes, of_x = shared_gate.shape[0], 640, 384
    dma = pltpu.SemaphoreType.DMA
    vmem = pltpu.VMEM
    routed = jax.ShapeDtypeStruct((hidden, model), BF16)
    return pl.pallas_call(
        layer_kernel,
        out_shape=(
            jax.ShapeDtypeStruct((tok_rows, width), BF16),
            jax.ShapeDtypeStruct(ids.shape, F32),
            routed,
            routed,
            routed,
            jax.ShapeDtypeStruct((chunk, lanes), BF16),
        ),
        in_specs=vmem_specs(4) + any_specs(3) + vmem_specs(3),
        out_specs=vmem_specs(2) + any_specs(3) + vmem_specs(1),
        scratch_shapes=[
            vmem((slots, tok_rows), BF16),
            vmem((3, slots, tok_rows), BF16),
            vmem((slots, 2 * width + 128), BF16),
            vmem((slots, 2 * width + 128), BF16),
            vmem((slots, 3 * width), BF16),
            vmem((slots, 3 * width), BF16),
            vmem((count, slots), BF16),
            vmem((count, 128), BF16),
            vmem((8, count, width), BF16),
            vmem((8, count, width), BF16),
            vmem((hidden, model), BF16),
            vmem((hidden, model), BF16),
            vmem((hidden, model), BF16),
            vmem((8, tok_rows, width), BF16),
            vmem((8, tok_rows, width), BF16),
            vmem((SIDE, SIDE, 2, chunk, lanes), BF16),
            vmem((tok_rows, lanes), F32),
            vmem((tok_rows, of_x), BF16),
            vmem((tok_rows, lanes - of_x), BF16),
            vmem((SIDE, SIDE, 2, chunk, lanes), BF16),
            vmem((SIDE, SIDE, chunk, lanes), BF16),
            vmem((4, 3, SIDE, 48, lanes), BF16),
            vmem((4, 3, 48, lanes), BF16),
            vmem((count, hidden), F32),
            vmem((count, hidden), F32),
            vmem((count, hidden), F32),
            vmem((count, hidden), BF16),
            vmem((count, hidden), BF16),
            vmem((count, hidden), BF16),
            vmem((hidden, count), BF16),
            vmem((hidden, count), BF16),
            vmem((hidden, count), BF16),
            vmem((16, width), BF16),
            vmem((8, count + 16, width), BF16),
            vmem((4, count + 16, width), BF16),
            vmem((4, count + 16, width), BF16),
            vmem((8, tok_rows, width), BF16),
            vmem((4, tok_rows, width), BF16),
            vmem((4, tok_rows, width), BF16),
            vmem((slots, width + 128), BF16),
            dma((5,)),
            dma((31,)),
            dma((31,)),
            dma((31,)),
            dma((31,)),
            dma((2, 2, 4)),
            dma((2, 2, 4)),
            dma((4, 2, 3)),
            dma((4, 2, 3)),
            dma((4, 2, 4)),
            dma((4, 2, 4)),
            dma((2, 2, 4)),
            dma((2, 2, 4)),
            dma,
            dma,
            dma((4, 2, 3)),
            dma((4, 2, 3)),
            dma((2, 2, 4)),
            dma((2, 2, 4)),
            dma((2, 2, 4)),
            dma((2, 2, 4)),
            dma((2, 3)),
            dma((31,)),
            dma((31,)),
        ],
        compiler_params=pltpu.CompilerParams(
            collective_id=0, has_side_effects=True, vmem_limit_bytes=62 * MIB
        ),
    )(ids, gates, tok, grad, w_gate, w_up, w_down, shared_gate, shared_up, shared_down)


PARTS = 2


def finish_kernel(
    tok, route, shared, in_gate, in_up, in_down,
    out_tok, out_route, out_gate, out_up, out_down, shared_gate, shared_up, shared_down,
):
    out_gate[...] = in_gate[...]
    out_up[...] = in_up[...]
    out_down[...] = in_down[...]

    @pl.when(pl.program_id(0) == 0)
    def _():
        out_tok[...] = tok[...]
        out_route[...] = route[...]
        units = shared_gate.shape[1]
        shared_gate[:, :128] = shared[:, :128]
        shared_gate[:, 128:] = shared[:, 256 : 256 + units - 128]
        shared_up[:, :128] = shared[:, 128:256]
        shared_up[:, 128:] = dot(shared[:, 256:384], one_hot(128, units - 128, 64)).astype(BF16)
        shared_down[:, :128] = shared[:, 384:512]
        shared_down[:, 128:] = shared[:, 512 : 512 + units - 128]


def finish(tok, route, shared, grads, shared_shapes):
    shapes = [tok, route, *grads, *shared_shapes]
    hidden, model = grads[0].shape

    def whole(part):
        return pl.BlockSpec(part.shape, lambda step: (0, 0))

    band = [pl.BlockSpec((hidden // PARTS, model), lambda step: (step, 0))] * 3
    return pl.pallas_call(
        finish_kernel,
        grid=(PARTS,),
        out_shape=tuple(jax.ShapeDtypeStruct(part.shape, part.dtype) for part in shapes),
        in_specs=[whole(tok), whole(route), whole(shared), *band],
        out_specs=[whole(tok), whole(route), *band, *map(whole, shared_shapes)],
        compiler_params=pltpu.CompilerParams(vmem_limit_bytes=62 * MIB),
    )(tok, route, shared, *grads)


def body(
    tokens, out_grad, expert_ids, gates, w_gate, w_up, w_down, shared_gate, shared_up, shared_down
):
    shared = (shared_gate, shared_up, shared_down.T)
    token_grad, route, grad_gate, grad_up, grad_down, grad_shared = layer(
        expert_ids.T, gates.T, tokens, out_grad, w_gate[0], w_up[0], w_down[0], *shared
    )
    token_grad, route, grad_gate, grad_up, grad_down, *grads = finish(
        token_grad, route, grad_shared, (grad_gate, grad_up, grad_down), shared
    )
    return (
        token_grad,
        route.T,
        grad_gate[None],
        grad_up[None],
        grad_down[None],
        grads[0],
        grads[1],
        grads[2].T,
    )


def solution(mesh):
    return jax.shard_map(
        body,
        mesh=mesh,
        in_specs=(
            P("seq", "exp"),
            P("seq", "exp"),
            P("seq", None),
            P("seq", None),
            P("seq", "exp", None),
            P("seq", "exp", None),
            P("seq", "exp", None),
            P("seq", "exp"),
            P("seq", "exp"),
            P("exp", "seq"),
        ),
        out_specs=(
            P("seq", "exp"),
            P("seq", None),
            P("seq", "exp", None),
            P("seq", "exp", None),
            P("seq", "exp", None),
            P("seq", "exp"),
            P("seq", "exp"),
            P("exp", "seq"),
        ),
        check_vma=False,
    )
```
